128 devices in a mesh: lat: 4 (over y_hi, core), lon: 32 (over x, y_lo, z).
Axes of the slice: x: 4, y: 4 (y_hi: 2, y_lo: 2; y = y_hi * 2 + y_lo), z: 4, core: 2. Of those that a mesh axis runs over, the one named last changes fastest.
Arguments:
- tokens: bfloat16 [4, 8, 48, 384, 384], P(None, None, 'lat', 'lon'), may hold values from -6 to 6
- w_qkv: bfloat16 [384, 1152], replicated, may hold values from -0.3125 to 0.3125
- w_proj: bfloat16 [384, 384], replicated, may hold values from -0.3125 to 0.3125
- w_up: bfloat16 [384, 1536], replicated, may hold values from -0.3125 to 0.3125
- w_down: bfloat16 [1536, 384], replicated, may hold values from -0.15625 to 0.15625
- w_merge: bfloat16 [1536, 768], replicated, may hold values from -0.15625 to 0.15625
- earth_bias: float32 [8, 4, 3312, 12], P('lat'), may hold values from -3 to 303
- position_index: int32 [144, 144], replicated, may hold values from 0 to 3311
- region_ids: int32 [8, 4, 144], P('lat'), may hold values from 0 to 2
Outputs:
- merged: bfloat16 [4, 8, 24, 192, 768], P(None, None, 'lat', 'lon')
The draws below stay inside these ranges and needn't reach their ends.
All inputs are finite; a program needn't handle non-finite values.
Results may differ from the reference program's by a relative error of at most 0.019.
Values may be sent and summed in bfloat16 or wider, within the bound.
A program may use at most 192 MiB of HBM per device.

```python
import jax
import jax.numpy as jnp
from jax import lax

C = 384
HEADS = 12
HEAD_DIM = 32
FFN = 1536
WZ = 2
WLAT = 6
WLON = 12
REGIONS = 3
ZL = 8
B = 4
WIN_TOK = 144
POS = 3312
LAT = 48
LON = 384
LATW = 8
ZW = 4


def draw_earth_bias(key, part):
    key = jax.random.fold_in(key, 7)
    base_key = jax.random.fold_in(key, 0)
    shape = (LATW, ZW, POS, HEADS)
    values = jnp.clip(jax.random.normal(base_key, shape, jnp.float32), -3.0, 3.0)
    return values


def touch_ends(entries, rng, smallest, top_value):
    extent = entries.shape
    spot = [jax.random.randint(jax.random.fold_in(rng, axis), (), 0, extent[axis]) for axis in range(len(extent))]
    entries = entries.at[tuple(spot)].set(smallest)
    longest = extent.index(max(extent))
    spot[longest] = (spot[longest] + 1) % extent[longest]
    return entries.at[tuple(spot)].set(top_value)


def shard_levels(stream_key, extent, cuts, low, largest):
    loudness, own = 1.0, jax.random.fold_in(stream_key, 6)
    for position, shards_of in cuts:
        draws = jnp.exp(jax.random.uniform(jax.random.fold_in(own, position), (shards_of,), jnp.float32, low / len(cuts), largest / len(cuts)))
        loudness = loudness * jnp.repeat(draws, extent[position] // shards_of).reshape([-1 if axis == position else 1 for axis in range(len(extent))])
    return loudness


def noise(rng, dims, deviation, limit, cuts=(), dtype=jnp.bfloat16):
    gain = shard_levels(rng, dims, cuts, -0.22, 0.18) if cuts else 1.0
    drawn = jax.random.normal(rng, dims, jnp.float32) * deviation * gain
    return jnp.minimum(jnp.maximum(drawn, -limit), limit).astype(dtype)


def setup_inputs(seed: int = 0) -> dict:
    arg_keys = jax.random.split(jax.random.key(seed), 10)
    tokens = noise(arg_keys[0], (B, ZL, LAT, LON, C), 1.0, 6.0, ((2, 4), (3, 32)))
    w_qkv = noise(arg_keys[1], (C, 3 * C), C ** -0.5, 0.3125)
    w_proj = noise(arg_keys[2], (C, C), C ** -0.5, 0.3125)
    w_up = noise(arg_keys[3], (C, FFN), C ** -0.5, 0.3125)
    w_down = noise(arg_keys[4], (FFN, C), FFN ** -0.5, 0.15625)
    w_merge = noise(arg_keys[5], (4 * C, 2 * C), (4 * C) ** -0.5, 0.15625)
    earth_bias = draw_earth_bias(jax.random.fold_in(arg_keys[9], 71), 0)
    position_index = touch_ends(jax.random.randint(arg_keys[7], (WIN_TOK, WIN_TOK), 0, POS), jax.random.fold_in(arg_keys[7], 1), 0, POS - 1).astype(jnp.int32)
    region_ids = touch_ends(jax.random.randint(arg_keys[8], (LATW, ZW, WIN_TOK), 0, REGIONS), jax.random.fold_in(arg_keys[8], 1), 0, REGIONS - 1).astype(jnp.int32)
    return {"tokens": tokens, "w_qkv": w_qkv, "w_proj": w_proj, "w_up": w_up, "w_down": w_down, "w_merge": w_merge, "earth_bias": earth_bias, "position_index": position_index, "region_ids": region_ids}


def layer_norm(values_in):
    center = values_in - lax.optimization_barrier(jnp.mean(values_in, axis=-1, keepdims=True))
    spread = lax.optimization_barrier(jnp.mean(center * center, axis=-1, keepdims=True))
    return center * lax.rsqrt(spread + 1e-05)

def to_windows(field):
    batch, levels, rows, cols, width = field.shape
    parts = field.reshape(batch, levels // WZ, WZ, rows // WLAT, WLAT, cols // WLON, WLON, width)
    parts = parts.transpose(3, 0, 1, 5, 2, 4, 6, 7)
    return parts.reshape(rows // WLAT, batch, levels // WZ, cols // WLON, WZ * WLAT * WLON, width)

def from_windows(windows, batch, levels, rows, cols):
    width = windows.shape[-1]
    parts = windows.reshape(rows // WLAT, batch, levels // WZ, cols // WLON, WZ, WLAT, WLON, width)
    parts = parts.transpose(1, 2, 4, 0, 5, 3, 6, 7)
    return parts.reshape(batch, levels, rows, cols, width)

def attend(band_windows, bias_table, region_row, position_index, w_qkv, w_proj):
    batch, zwin, owin, slots, width = band_windows.shape
    projected = jnp.dot(band_windows.reshape(-1, width), w_qkv, preferred_element_type=jnp.float32).astype(jnp.bfloat16)
    projected = projected.reshape(batch, zwin, owin, slots, 3, HEADS, HEAD_DIM)
    queries = projected[:, :, :, :, 0].astype(jnp.float32)
    key_block = projected[:, :, :, :, 1].astype(jnp.float32)
    value_block = projected[:, :, :, :, 2].astype(jnp.float32)
    scores = jnp.einsum('bzoqhd,bzokhd->bzohqk', queries, key_block) * HEAD_DIM ** (-0.5)
    bias_block = jnp.take(bias_table, position_index, axis=1).transpose(0, 3, 1, 2)
    allowed = region_row[:, :, None] == region_row[:, None, :]
    scores = scores + bias_block[None, :, None]
    scores = jnp.where(allowed[None, :, None, None], scores, -1000000000.0)
    row_max = lax.optimization_barrier(jnp.max(scores, axis=-1, keepdims=True))
    raised = jnp.exp(scores - row_max)
    attn_probs = (raised / lax.optimization_barrier(jnp.sum(raised, axis=-1, keepdims=True))).astype(jnp.bfloat16)
    context = jnp.einsum('bzohqk,bzokhd->bzoqhd', attn_probs.astype(jnp.float32), value_block).astype(jnp.bfloat16)
    result_rows = jnp.dot(context.reshape(-1, width), w_proj, preferred_element_type=jnp.float32).astype(jnp.bfloat16)
    return result_rows.reshape(batch, zwin, owin, slots, width)

def feed_merge(hidden, w_up, w_down, w_merge):
    lead = hidden.shape[:-3]
    rows, cols, width = hidden.shape[-3:]
    flat = hidden.reshape(-1, width)
    normed = layer_norm(flat.astype(jnp.float32)).astype(jnp.bfloat16)
    inner = jax.nn.gelu(jnp.dot(normed, w_up, preferred_element_type=jnp.float32), approximate=False).astype(jnp.bfloat16)
    block_out = (flat.astype(jnp.float32) + jnp.dot(inner, w_down, preferred_element_type=jnp.float32)).astype(jnp.bfloat16)
    depth = len(lead)
    grid = block_out.reshape(lead + (rows // 2, 2, cols // 2, 2, width))
    order = tuple(range(depth)) + (depth, depth + 2, depth + 1, depth + 3, depth + 4)
    grouped = grid.transpose(order).reshape(-1, 4 * width)
    grouped_norm = layer_norm(grouped.astype(jnp.float32)).astype(jnp.bfloat16)
    result_rows = jnp.dot(grouped_norm, w_merge, preferred_element_type=jnp.float32).astype(jnp.bfloat16)
    return result_rows.reshape(lead + (rows // 2, cols // 2, 2 * width))

def reference(tokens, w_qkv, w_proj, w_up, w_down, w_merge, earth_bias, position_index, region_ids):
    shifted = jnp.roll(tokens, (-(WZ // 2), -(WLAT // 2), -(WLON // 2)), axis=(1, 2, 3))
    normed = layer_norm(shifted.astype(jnp.float32)).astype(jnp.bfloat16)
    windows = to_windows(normed)

    def per_band(pack):
        return attend(pack[0], pack[1], pack[2], position_index, w_qkv, w_proj)
    attended = lax.map(per_band, (windows, earth_bias, region_ids))
    restored = from_windows(attended, B, ZL, LAT, LON)
    restored = jnp.roll(restored, (WZ // 2, WLAT // 2, WLON // 2), axis=(1, 2, 3))
    hidden = (tokens.astype(jnp.float32) + restored.astype(jnp.float32)).astype(jnp.bfloat16)

    def per_layer(layer_rows):
        return feed_merge(layer_rows, w_up, w_down, w_merge)
    merged = lax.map(per_layer, hidden.reshape(B * ZL, LAT, LON, C))
    return merged.reshape(B, ZL, LAT // 2, LON // 2, 2 * C)
```

```python
import functools

import jax
import jax.numpy as jnp
import numpy as np
from jax import lax
from jax.experimental import pallas as pl
from jax.experimental.pallas import tpu as pltpu
from jax.sharding import PartitionSpec as P

HEADS = 12
HEAD_DIM = 32
C = 384
FFN = 1536
ZL = 8
ZW = 4
HALF = 72
SLOTS = 144
CELLS = 288
PIECE = 144
LOG2E = 1.4426950408889634
BF = jnp.bfloat16
F32 = jnp.float32


def passed_along(block, axis, distance):
    devices = range(lax.axis_size(axis))
    route = [((i - distance) % len(devices), i) for i in devices]
    return lax.ppermute(block, axis, route)


def window_order():
    one_hot = np.zeros((CELLS, CELLS), np.float32)
    for zw in range(ZW):
        for z in range(2):
            for r in range(6):
                for c in range(6):
                    one_hot[zw * HALF + z * 36 + r * 6 + c, (r * 6 + c) * ZL + (2 * zw + 1 + z) % ZL] = 1.0
    return one_hot


def slot_order():
    order = []
    for side in range(2):
        for z in range(2):
            for r in range(6):
                for c in range(6):
                    order.append((z * 6 + r) * 12 + side * 6 + c)
    return np.array(order, np.int32)


def normalized(x):
    width = x.shape[-1]
    center = x - jnp.sum(x, axis=-1, keepdims=True) * (1.0 / width)
    spread = jnp.sum(center * center, axis=-1, keepdims=True) * (1.0 / width)
    return center * lax.rsqrt(spread + 1e-05)


def dot(a, b):
    return jnp.dot(a, b, preferred_element_type=F32)


def full(shape):
    return pl.BlockSpec(shape, lambda *i: (0,) * len(shape))


def pack_kernel(tok_ref, first_ref, mid_ref, last_ref):
    for piece in range(4):
        x = normalized(tok_ref[0, 3 * piece : 3 * piece + 3].astype(F32))
        for side in range(2):
            part = x[:, 6 * side : 6 * side + 6].reshape(PIECE, C).astype(BF)
            if piece == 0:
                first_ref[side, 0] = part
            elif piece == 3:
                last_ref[side, 0] = part
            else:
                mid_ref[side, 0, piece - 1] = part


def pack(tok):
    batch = tok.shape[0]
    return pl.pallas_call(
        pack_kernel,
        grid=(batch,),
        in_specs=[pl.BlockSpec((1, 12, 12, ZL, C), lambda b: (b, 0, 0, 0, 0))],
        out_specs=[
            pl.BlockSpec((2, 1, PIECE, C), lambda b: (0, b, 0, 0)),
            pl.BlockSpec((2, 1, 2, PIECE, C), lambda b: (0, b, 0, 0, 0)),
            pl.BlockSpec((2, 1, PIECE, C), lambda b: (0, b, 0, 0)),
        ],
        out_shape=[
            jax.ShapeDtypeStruct((2, batch, PIECE, C), BF),
            jax.ShapeDtypeStruct((2, batch, 2, PIECE, C), BF),
            jax.ShapeDtypeStruct((2, batch, PIECE, C), BF),
        ],
        cost_estimate=pl.CostEstimate(flops=20_000_000, bytes_accessed=8_000_000, transcendentals=0),
        compiler_params=pltpu.CompilerParams(vmem_limit_bytes=32 << 20),
        name="pack",
    )(tok)


ROWS_AT_ONCE = 8
TYPE_HEADS = 96
TABLE = 3328
UNROLL = 48


def bias_kernel(index_ref, table_ref, region_ref, region_col_ref, out_ref, rows, picked, left, right):
    step = pl.program_id(0)

    @pl.when(step == 0)
    def _():
        for c in range(TABLE // 128):
            rows[128 * c : 128 * (c + 1), :] = table_ref[:, 128 * c : 128 * (c + 1)].T

    start = step * (ROWS_AT_ONCE * SLOTS)

    def pick(i, carry):
        base = pl.multiple_of(i * UNROLL, 8)
        for k in range(UNROLL):
            picked[pl.ds(base + k, 1), :] = rows[pl.ds(index_ref[start + base + k], 1), :]
        return carry

    lax.fori_loop(0, ROWS_AT_ONCE * SLOTS // UNROLL, pick, 0)
    for s in range(ROWS_AT_ONCE):
        left[TYPE_HEADS * s : TYPE_HEADS * (s + 1), :] = picked[SLOTS * s : SLOTS * s + 128, :].T[:TYPE_HEADS]
        right[TYPE_HEADS * s : TYPE_HEADS * (s + 1), :16] = picked[SLOTS * s + 128 : SLOTS * (s + 1), :].T[:TYPE_HEADS]
    for lw in range(2):
        for zw in range(ZW):
            kind = lw * ZW + zw
            same = region_col_ref[:, kind : kind + 1] == region_ref[kind : kind + 1, :]
            for h in range(HEADS):
                source = (lw * HEADS + h) * ZW + zw
                place = kind * HEADS + h
                out_ref[place, :, :128] = jnp.where(
                    same[:, :128], left[pl.ds(source, ROWS_AT_ONCE, stride=TYPE_HEADS), :] * LOG2E, -1e9
                )
                out_ref[place, :, 128:] = jnp.where(
                    same[:, 128:], right[pl.ds(source, ROWS_AT_ONCE, stride=TYPE_HEADS), :][:, :16] * LOG2E, -1e9
                )


def bias_of(earth_bias, position_index, region_ids):
    order = slot_order()
    index = position_index[order][:, order].reshape(-1)
    table = jnp.transpose(earth_bias, (0, 3, 1, 2)).reshape(TYPE_HEADS, -1)
    table = jnp.pad(table, ((0, 128 - TYPE_HEADS), (0, TABLE - table.shape[1])))
    region = region_ids.reshape(2 * ZW, SLOTS)[:, order]
    return pl.pallas_call(
        bias_kernel,
        grid_spec=pltpu.PrefetchScalarGridSpec(
            num_scalar_prefetch=1,
            grid=(SLOTS // ROWS_AT_ONCE,),
            in_specs=[
                full((128, TABLE)),
                full((2 * ZW, SLOTS)),
                pl.BlockSpec((ROWS_AT_ONCE, 2 * ZW), lambda i, _: (i, 0)),
            ],
            out_specs=pl.BlockSpec((TYPE_HEADS, ROWS_AT_ONCE, SLOTS), lambda i, _: (0, i, 0)),
            scratch_shapes=[
                pltpu.VMEM((TABLE, 128), F32),
                pltpu.VMEM((ROWS_AT_ONCE * SLOTS, 128), F32),
                pltpu.VMEM((ROWS_AT_ONCE * TYPE_HEADS, 128), F32),
                pltpu.VMEM((ROWS_AT_ONCE * TYPE_HEADS, 128), F32),
            ],
        ),
        out_shape=jax.ShapeDtypeStruct((TYPE_HEADS, SLOTS, SLOTS), F32),
        cost_estimate=pl.CostEstimate(flops=20_000_000, bytes_accessed=70_000_000, transcendentals=0),
        compiler_params=pltpu.CompilerParams(vmem_limit_bytes=32 << 20),
        name="bias",
    )(index, table, region, region.T)


def attend_kernel(
    own_a, own_b, right_a, right_b, left_a, left_b, order_ref, back_ref, w_qkv_ref, w_proj_ref, bias_ref,
    out_a, out_b, own_scr, halo_scr, ctx_scr,
):
    order = order_ref[...]

    def windows(top, bottom):
        return dot(order, jnp.concatenate([top, bottom], axis=0)).astype(BF)

    own = jnp.concatenate([windows(own_a[1, 0], own_b[1, 0]), windows(own_a[0, 0], own_b[0, 0])], axis=0)
    own_scr[...] = dot(own, w_qkv_ref[...])
    halo = jnp.concatenate([windows(right_a[0], right_b[0]), windows(left_a[0], left_b[0])], axis=0)
    halo_scr[...] = dot(halo, w_qkv_ref[:, C:])
    lane_head = lax.broadcasted_iota(jnp.int32, (1, 128), 1) // HEAD_DIM
    masks = [lane_head == h for h in range(4)]
    ones = jnp.ones((SLOTS, 128), BF)

    def window(zw, carry):
        for side in range(2):
            rows = pl.ds(pl.multiple_of(side * CELLS + zw * HALF, 8), HALF)
            for g in range(3):
                lanes = slice(128 * g, 128 * g + 128)
                klanes = slice(C + 128 * g, C + 128 * g + 128)
                vlanes = slice(2 * C + 128 * g, 2 * C + 128 * g + 128)
                q = own_scr[rows, lanes] * (HEAD_DIM ** (-0.5) * LOG2E)
                stacked = jnp.concatenate([jnp.where(m, q, 0.0) for m in masks], axis=0).astype(BF)
                k = [own_scr[rows, klanes], halo_scr[rows, lanes]]
                v = [own_scr[rows, vlanes], halo_scr[rows, klanes]]
                if side == 1:
                    k, v = k[::-1], v[::-1]
                keys = jnp.concatenate(k, axis=0).astype(BF)
                values = jnp.concatenate([jnp.concatenate(v, axis=0).astype(BF), ones], axis=1)
                scores = lax.dot_general(stacked, keys, (((1,), (1,)), ((), ())), preferred_element_type=F32)
                bias = bias_ref[pl.ds(zw * HEADS + 4 * g, 4), side * HALF : (side + 1) * HALF, :]
                scores = scores + bias.reshape(4 * HALF, SLOTS)
                raised = jnp.exp2(scores - jnp.max(scores, axis=-1, keepdims=True)).astype(BF)
                both = dot(raised, values)
                top, total = both[:HALF, :128], both[:HALF, 128:]
                for h in range(1, 4):
                    top = jnp.where(masks[h], both[h * HALF : (h + 1) * HALF, :128], top)
                    total = jnp.where(masks[h], both[h * HALF : (h + 1) * HALF, 128:], total)
                ctx_scr[rows, lanes] = top / total
        return carry

    lax.fori_loop(0, ZW, window, 0)
    back = back_ref[...]
    for side in range(2):
        natural = dot(back, ctx_scr[CELLS * side : CELLS * (side + 1), :].astype(BF)).astype(BF)
        result = dot(natural, w_proj_ref[...]).astype(BF)
        out_a[1 - side, 0] = result[:PIECE]
        out_b[1 - side, 0] = result[PIECE:]


def attend(own, right, left, order, w_qkv, w_proj, bias, lw):
    batch = own[0][0].shape[1]
    arrays, specs = [], []
    for pair, sides in ((own, True), (right, False), (left, False)):
        for array, piece in pair:
            arrays.append(array)
            lead = (2, 1) if sides else (1,)

            def place(b, sides=sides, piece=piece):
                where = (0, b) if sides else (b,)
                return where + (() if piece is None else (piece,)) + (0, 0)

            specs.append(pl.BlockSpec(lead + (() if piece is None else (None,)) + (PIECE, C), place))
    out = jax.ShapeDtypeStruct((2, batch, PIECE, C), BF)
    out_spec = pl.BlockSpec((2, 1, PIECE, C), lambda b: (0, b, 0, 0))
    return pl.pallas_call(
        attend_kernel,
        grid=(batch,),
        in_specs=specs
        + [
            full((CELLS, CELLS)),
            full((CELLS, CELLS)),
            full((C, 3 * C)),
            full((C, C)),
            pl.BlockSpec((ZW * HEADS, SLOTS, SLOTS), lambda b: (lw, 0, 0)),
        ],
        out_specs=[out_spec, out_spec],
        out_shape=[out, out],
        scratch_shapes=[
            pltpu.VMEM((2 * CELLS, 3 * C), F32),
            pltpu.VMEM((2 * CELLS, 2 * C), F32),
            pltpu.VMEM((2 * CELLS, C), F32),
        ],
        cost_estimate=pl.CostEstimate(flops=20_000_000_000, bytes_accessed=16_000_000, transcendentals=4_000_000),
        compiler_params=pltpu.CompilerParams(vmem_limit_bytes=56 << 20),
        name="attend",
    )(*arrays, jnp.asarray(order, BF), jnp.asarray(order.T, BF), w_qkv, w_proj, bias)


STRIP = 4


def feed_kernel(tok_ref, first_ref, mid_a, mid_b, last_ref, w_up_ref, w_down_ref, w_merge_ref, out_ref, hidden_scr):
    for piece, ref in enumerate((first_ref, mid_a, mid_b, last_ref)):
        for side in range(2):
            rows, cols = slice(3 * piece, 3 * piece + 3), slice(6 * side, 6 * side + 6)
            tok = tok_ref[0, rows, cols].astype(F32)
            attended = ref[side, 0].astype(F32).reshape(3, 6, ZL, C)
            hidden_scr[rows, cols] = (tok + attended).astype(BF).astype(F32)

    def strip(i, carry):
        hidden = hidden_scr[pl.ds(i * STRIP, STRIP)].reshape(STRIP * 12 * ZL, C)
        up = dot(normalized(hidden).astype(BF), w_up_ref[...])
        inner = (0.5 * up * (1.0 + lax.erf(up * 0.7071067811865476))).astype(BF)
        block = (hidden + dot(inner, w_down_ref[...])).astype(BF).astype(F32)
        block = block.reshape(STRIP // 2, 2, 6, 2, ZL, C)
        grouped = jnp.concatenate([block[:, p // 2, :, p % 2] for p in range(4)], axis=-1)
        grouped = normalized(grouped.reshape(STRIP // 2 * 6 * ZL, 4 * C)).astype(BF)
        merged = dot(grouped, w_merge_ref[...])
        out_ref[0, pl.ds(i * (STRIP // 2), STRIP // 2)] = merged.reshape(STRIP // 2, 6, ZL, 2 * C).astype(BF)
        return carry

    lax.fori_loop(0, 12 // STRIP, strip, 0)


def feed(tok, first, mid_a, mid_b, last, w_up, w_down, w_merge):
    batch = tok.shape[0]
    piece = pl.BlockSpec((2, 1, PIECE, C), lambda b: (0, b, 0, 0))
    return pl.pallas_call(
        feed_kernel,
        grid=(batch,),
        in_specs=[
            pl.BlockSpec((1, 12, 12, ZL, C), lambda b: (b, 0, 0, 0, 0)),
            piece,
            piece,
            piece,
            piece,
            full((C, FFN)),
            full((FFN, C)),
            full((4 * C, 2 * C)),
        ],
        out_specs=pl.BlockSpec((1, 6, 6, ZL, 2 * C), lambda b: (b, 0, 0, 0, 0)),
        out_shape=jax.ShapeDtypeStruct((batch, 6, 6, ZL, 2 * C), BF),
        scratch_shapes=[pltpu.VMEM((12, 12, ZL, C), F32)],
        cost_estimate=pl.CostEstimate(flops=14_000_000_000, bytes_accessed=14_000_000, transcendentals=7_000_000),
        compiler_params=pltpu.CompilerParams(vmem_limit_bytes=56 << 20),
        name="feed",
    )(tok, first, mid_a, mid_b, last, w_up, w_down, w_merge)


def on_device(tokens, w_qkv, w_proj, w_up, w_down, w_merge, earth_bias, position_index, region_ids):
    tok = jnp.transpose(tokens, (0, 2, 3, 1, 4))
    order = window_order()
    first, mid, last = pack(tok)
    below = passed_along(first, "lat", -1)
    right_mid = passed_along(mid[0], "lon", -1)
    left_mid = passed_along(mid[1], "lon", 1)
    right_last = passed_along(last[0], "lon", -1)
    left_last = passed_along(last[1], "lon", 1)
    right_below = passed_along(below[0], "lon", -1)
    left_below = passed_along(below[1], "lon", 1)
    bias = bias_of(earth_bias, position_index, region_ids)
    mid_a, mid_b = attend(
        ((mid, 0), (mid, 1)), ((right_mid, 0), (right_mid, 1)), ((left_mid, 0), (left_mid, 1)),
        order, w_qkv, w_proj, bias, 0,
    )
    last_out, below_out = attend(
        ((last, None), (below, None)), ((right_last, None), (right_below, None)),
        ((left_last, None), (left_below, None)), order, w_qkv, w_proj, bias, 1,
    )
    first_out = passed_along(below_out, "lat", 1)
    merged = feed(tok, first_out, mid_a, mid_b, last_out, w_up, w_down, w_merge)
    return jnp.transpose(merged, (0, 3, 1, 2, 4))


def solution(mesh):
    in_specs = (
        P(None, None, "lat", "lon", None),
        P(),
        P(),
        P(),
        P(),
        P(),
        P("lat", None, None, None),
        P(),
        P("lat", None, None),
    )
    out_specs = P(None, None, "lat", "lon", None)
    return jax.shard_map(
        on_device, mesh=mesh, in_specs=in_specs, out_specs=out_specs, check_vma=False
    )
```

```python
import functools

import jax
import jax.numpy as jnp
import numpy as np
from jax import lax
from jax.experimental import pallas as pl
from jax.experimental.pallas import tpu as pltpu
from jax.sharding import PartitionSpec as P

HEADS = 12
HEAD_DIM = 32
C = 384
FFN = 1536
ZL = 8
ZW = 4
HALF = 72
SLOTS = 144
CELLS = 288
PIECE = 144
LOG2E = 1.4426950408889634
BF = jnp.bfloat16
F32 = jnp.float32


def passed_along(block, axis, distance):
    devices = range(lax.axis_size(axis))
    route = [((i - distance) % len(devices), i) for i in devices]
    return lax.ppermute(block, axis, route)


def window_order():
    one_hot = np.zeros((CELLS, CELLS), np.float32)
    for zw in range(ZW):
        for z in range(2):
            for r in range(6):
                for c in range(6):
                    one_hot[zw * HALF + z * 36 + r * 6 + c, (r * 6 + c) * ZL + (2 * zw + 1 + z) % ZL] = 1.0
    return one_hot


def normalized(x):
    width = x.shape[-1]
    center = x - jnp.sum(x, axis=-1, keepdims=True) * (1.0 / width)
    spread = jnp.sum(center * center, axis=-1, keepdims=True) * (1.0 / width)
    return center * lax.rsqrt(spread + 1e-05)


def dot(a, b):
    return jnp.dot(a, b, preferred_element_type=F32)


def full(shape):
    return pl.BlockSpec(shape, lambda *i: (0,) * len(shape))


def pack_kernel(tok_ref, first_ref, mid_left, mid_right, last_left, last_right):
    for piece in range(4):
        x = normalized(tok_ref[0, 3 * piece : 3 * piece + 3].astype(F32))
        for side in range(2):
            part = x[:, 6 * side : 6 * side + 6].reshape(PIECE, C).astype(BF)
            if piece == 0:
                first_ref[side, 0] = part
            elif piece == 3:
                (last_left, last_right)[side][0] = part
            else:
                (mid_left, mid_right)[side][0, piece - 1] = part


def pack(tok):
    batch = tok.shape[0]
    return pl.pallas_call(
        pack_kernel,
        grid=(batch,),
        in_specs=[pl.BlockSpec((1, 12, 12, ZL, C), lambda b: (b, 0, 0, 0, 0))],
        out_specs=[pl.BlockSpec((2, 1, PIECE, C), lambda b: (0, b, 0, 0))]
        + [pl.BlockSpec((1, 2, PIECE, C), lambda b: (b, 0, 0, 0))] * 2
        + [pl.BlockSpec((1, PIECE, C), lambda b: (b, 0, 0))] * 2,
        out_shape=[jax.ShapeDtypeStruct((2, batch, PIECE, C), BF)]
        + [jax.ShapeDtypeStruct((batch, 2, PIECE, C), BF)] * 2
        + [jax.ShapeDtypeStruct((batch, PIECE, C), BF)] * 2,
        cost_estimate=pl.CostEstimate(flops=20_000_000, bytes_accessed=8_000_000, transcendentals=0),
        compiler_params=pltpu.CompilerParams(vmem_limit_bytes=60 << 20),
        name="pack",
    )(tok)


ROWS_AT_ONCE = 8
TYPE_HEADS = 96
PITCH = 97
TABLE = 3328


def bias_kernel(side, index_ref, table_ref, region_ref, region_col_ref, out_ref, rows, picked, left, right):
    step = pl.program_id(0)

    @pl.when(step == 0)
    def _():
        for c in range(TABLE // 128):
            rows[128 * c : 128 * (c + 1), :] = table_ref[:, 128 * c : 128 * (c + 1)].T

    def pick(i, carry):
        row, half = step * ROWS_AT_ONCE + i // 2, i % 2
        start = ((row // 6) * 12 + side * 6 + row % 6) * SLOTS + half * 6
        base = pl.multiple_of(i * HALF, 8)
        for k in range(HALF):
            picked[pl.ds(base + k, 1), :] = rows[pl.ds(index_ref[start + k // 6 * 12 + k % 6], 1), :]
        return carry

    lax.fori_loop(0, ROWS_AT_ONCE * 2, pick, 0)
    for s in range(ROWS_AT_ONCE):
        left[PITCH * s : PITCH * s + TYPE_HEADS, :] = picked[SLOTS * s : SLOTS * s + 128, :].T[:TYPE_HEADS]
        right[PITCH * s : PITCH * s + TYPE_HEADS, :16] = picked[SLOTS * s + 128 : SLOTS * (s + 1), :].T[:TYPE_HEADS]
    for lw in range(2):
        for zw in range(ZW):
            kind = lw * ZW + zw
            same = region_col_ref[:, kind : kind + 1] == region_ref[kind : kind + 1, :]
            for h in range(HEADS):
                source = (lw * HEADS + h) * ZW + zw
                place = kind * HEADS + h
                out_ref[place, :, :128] = jnp.where(
                    same[:, :128], left[pl.ds(source, ROWS_AT_ONCE, stride=PITCH), :] * LOG2E, -1e9
                )
                out_ref[place, :, 128:] = jnp.where(
                    same[:, 128:], right[pl.ds(source, ROWS_AT_ONCE, stride=PITCH), :][:, :16] * LOG2E, -1e9
                )


def slot_order():
    return np.arange(SLOTS, dtype=np.int32).reshape(12, 2, 6).transpose(1, 0, 2).reshape(-1)


def bias_inputs(earth_bias, position_index, region_ids):
    index = position_index.reshape(-1)
    table = jnp.transpose(earth_bias, (0, 3, 1, 2)).reshape(TYPE_HEADS, -1)
    table = jnp.pad(table, ((0, 128 - TYPE_HEADS), (0, TABLE - table.shape[1])))
    region = region_ids.reshape(2 * ZW, SLOTS)[:, slot_order()]
    return index, table, region, region.T


def bias_of(inputs, side):
    index, table, region, region_col = inputs
    steps = HALF // ROWS_AT_ONCE
    return pl.pallas_call(
        functools.partial(bias_kernel, side),
        grid_spec=pltpu.PrefetchScalarGridSpec(
            num_scalar_prefetch=1,
            grid=(steps,),
            in_specs=[
                full((128, TABLE)),
                full((2 * ZW, SLOTS)),
                pl.BlockSpec((ROWS_AT_ONCE, 2 * ZW), lambda i, _: (side * steps + i, 0)),
            ],
            out_specs=pl.BlockSpec((TYPE_HEADS, ROWS_AT_ONCE, SLOTS), lambda i, _: (0, i, 0)),
            scratch_shapes=[
                pltpu.VMEM((TABLE, 128), F32),
                pltpu.VMEM((ROWS_AT_ONCE * SLOTS, 128), F32),
                pltpu.VMEM((ROWS_AT_ONCE * PITCH, 128), F32),
                pltpu.VMEM((ROWS_AT_ONCE * PITCH, 128), F32),
            ],
        ),
        out_shape=jax.ShapeDtypeStruct((TYPE_HEADS, HALF, SLOTS), F32),
        cost_estimate=pl.CostEstimate(flops=20_000_000, bytes_accessed=50_000_000, transcendentals=0),
        compiler_params=pltpu.CompilerParams(vmem_limit_bytes=60 << 20),
        name="bias",
    )(index, table, region, region_col)


def attend_kernel(
    lower_a, lower_b, upper_a, upper_b, right_a, right_b, left_a, left_b, order_ref, back_ref, w_qkv_ref, w_proj_ref, *rest
):
    bias_refs, (out_a, out_b, own_scr, halo_scr, ctx_scr) = rest[:2], rest[2:]
    order = order_ref[...]

    def windows(top, bottom):
        return dot(order, jnp.concatenate([top, bottom], axis=0)).astype(BF)

    own = jnp.concatenate([windows(upper_a[0], upper_b[0]), windows(lower_a[0], lower_b[0])], axis=0)
    own_scr[...] = dot(own, w_qkv_ref[...])
    halo = jnp.concatenate([windows(right_a[0], right_b[0]), windows(left_a[0], left_b[0])], axis=0)
    halo_scr[...] = dot(halo, w_qkv_ref[:, C:])
    lane_head = lax.broadcasted_iota(jnp.int32, (1, 128), 1) // HEAD_DIM
    masks = [lane_head == h for h in range(4)]
    ones = jnp.ones((SLOTS, 128), BF)

    for zw in range(ZW):
        for side in range(2):
            rows = slice(side * CELLS + zw * HALF, side * CELLS + (zw + 1) * HALF)
            for g in range(3):
                lanes = slice(128 * g, 128 * g + 128)
                klanes = slice(C + 128 * g, C + 128 * g + 128)
                vlanes = slice(2 * C + 128 * g, 2 * C + 128 * g + 128)
                q = own_scr[rows, lanes] * (HEAD_DIM ** (-0.5) * LOG2E)
                stacked = jnp.concatenate([jnp.where(m, q, 0.0) for m in masks], axis=0).astype(BF)
                k = [own_scr[rows, klanes], halo_scr[rows, lanes]]
                v = [own_scr[rows, vlanes], halo_scr[rows, klanes]]
                if side == 1:
                    k, v = k[::-1], v[::-1]
                keys = jnp.concatenate(k, axis=0).astype(BF)
                values = jnp.concatenate([jnp.concatenate(v, axis=0).astype(BF), ones], axis=1)
                scores = lax.dot_general(stacked, keys, (((1,), (1,)), ((), ())), preferred_element_type=F32)
                bias = bias_refs[side][zw * HEADS + 4 * g : zw * HEADS + 4 * g + 4]
                scores = scores + bias.reshape(4 * HALF, SLOTS)
                raised = jnp.exp2(scores - jnp.max(scores, axis=-1, keepdims=True)).astype(BF)
                both = dot(raised, values)
                top, total = both[:HALF, :128], both[:HALF, 128:]
                for h in range(1, 4):
                    top = jnp.where(masks[h], both[h * HALF : (h + 1) * HALF, :128], top)
                    total = jnp.where(masks[h], both[h * HALF : (h + 1) * HALF, 128:], total)
                ctx_scr[rows, lanes] = top / total
    back = back_ref[...]
    for side in range(2):
        natural = dot(back, ctx_scr[CELLS * side : CELLS * (side + 1), :].astype(BF)).astype(BF)
        result = dot(natural, w_proj_ref[...]).astype(BF)
        out_a[1 - side, 0] = result[:PIECE]
        out_b[1 - side, 0] = result[PIECE:]


def attend(streams, order, w_qkv, w_proj, bias, lw):
    batch = streams[-1][0].shape[0]
    arrays, specs = [], []
    for array, dim, index in streams:
        arrays.append(array)
        if dim is None:
            specs.append(pl.BlockSpec((1, PIECE, C), lambda b: (b, 0, 0)))
        elif dim == 0:
            specs.append(pl.BlockSpec((None, 1, PIECE, C), lambda b, i=index: (i, b, 0, 0)))
        else:
            specs.append(pl.BlockSpec((1, None, PIECE, C), lambda b, i=index: (b, i, 0, 0)))
    out = jax.ShapeDtypeStruct((2, batch, PIECE, C), BF)
    out_spec = pl.BlockSpec((2, 1, PIECE, C), lambda b: (0, b, 0, 0))
    return pl.pallas_call(
        attend_kernel,
        grid=(batch,),
        in_specs=specs
        + [
            full((CELLS, CELLS)),
            full((CELLS, CELLS)),
            full((C, 3 * C)),
            full((C, C)),
            pl.BlockSpec((ZW * HEADS, HALF, SLOTS), lambda b: (lw, 0, 0)),
            pl.BlockSpec((ZW * HEADS, HALF, SLOTS), lambda b: (lw, 0, 0)),
        ],
        out_specs=[out_spec, out_spec],
        out_shape=[out, out],
        scratch_shapes=[
            pltpu.VMEM((2 * CELLS, 3 * C), F32),
            pltpu.VMEM((2 * CELLS, 2 * C), F32),
            pltpu.VMEM((2 * CELLS, C), F32),
        ],
        cost_estimate=pl.CostEstimate(flops=20_000_000_000, bytes_accessed=16_000_000, transcendentals=4_000_000),
        compiler_params=pltpu.CompilerParams(vmem_limit_bytes=60 << 20),
        name="attend",
    )(*arrays, jnp.asarray(order, BF), jnp.asarray(order.T, BF), w_qkv, w_proj, *bias)


CHUNK = 768


def feed_kernel(tok_ref, first_ref, mid_a, mid_b, last_ref, w_up_ref, w_down_ref, w_merge_ref, out_ref, hidden_scr):
    for piece, ref in enumerate((first_ref, mid_a, mid_b, last_ref)):
        for side in range(2):
            rows, cols = slice(3 * piece, 3 * piece + 3), slice(6 * side, 6 * side + 6)
            tok = tok_ref[0, rows, cols].astype(F32)
            attended = ref[side, 0].astype(F32).reshape(3, 6, ZL, C)
            hidden_scr[rows, cols] = (tok + attended).astype(BF).astype(F32)

    hidden = hidden_scr[...].reshape(12 * 12 * ZL, C)
    normed = normalized(hidden).astype(BF)
    block = hidden
    for f in range(0, FFN, CHUNK):
        up = dot(normed, w_up_ref[:, f : f + CHUNK])
        inner = (0.5 * up * (1.0 + lax.erf(up * 0.7071067811865476))).astype(BF)
        block = block + dot(inner, w_down_ref[f : f + CHUNK])
    block = block.astype(BF).astype(F32).reshape(6, 2, 6, 2, ZL, C)
    grouped = jnp.concatenate([block[:, p // 2, :, p % 2] for p in range(4)], axis=-1)
    grouped = normalized(grouped.reshape(36 * ZL, 4 * C)).astype(BF)
    out_ref[0] = dot(grouped, w_merge_ref[...]).reshape(6, 6, ZL, 2 * C).astype(BF)


def feed(tok, first, mid_a, mid_b, last, w_up, w_down, w_merge):
    batch = tok.shape[0]
    piece = pl.BlockSpec((2, 1, PIECE, C), lambda b: (0, b, 0, 0))
    return pl.pallas_call(
        feed_kernel,
        grid=(batch,),
        in_specs=[
            pl.BlockSpec((1, 12, 12, ZL, C), lambda b: (b, 0, 0, 0, 0)),
            piece,
            piece,
            piece,
            piece,
            full((C, FFN)),
            full((FFN, C)),
            full((4 * C, 2 * C)),
        ],
        out_specs=pl.BlockSpec((1, 6, 6, ZL, 2 * C), lambda b: (b, 0, 0, 0, 0)),
        out_shape=jax.ShapeDtypeStruct((batch, 6, 6, ZL, 2 * C), BF),
        scratch_shapes=[pltpu.VMEM((12, 12, ZL, C), F32)],
        cost_estimate=pl.CostEstimate(flops=14_000_000_000, bytes_accessed=14_000_000, transcendentals=7_000_000),
        compiler_params=pltpu.CompilerParams(vmem_limit_bytes=60 << 20),
        name="feed",
    )(tok, first, mid_a, mid_b, last, w_up, w_down, w_merge)


def on_device(tokens, w_qkv, w_proj, w_up, w_down, w_merge, earth_bias, position_index, region_ids):
    tok = jnp.transpose(tokens, (0, 2, 3, 1, 4))
    order = window_order()
    first, mid_left, mid_right, last_left, last_right = pack(tok)
    inputs = bias_inputs(earth_bias, position_index, region_ids)
    below = passed_along(first, "lat", -1)
    next_last = passed_along(last_left, "lon", -1)
    prev_last = passed_along(last_right, "lon", 1)
    bias_left = bias_of(inputs, 0)
    below, mid_left, mid_right, bias_left, inputs = lax.optimization_barrier(
        (below, mid_left, mid_right, bias_left, inputs)
    )
    below_left, below_right = below[0], below[1]
    next_below = passed_along(below_left, "lon", -1)
    prev_below = passed_along(below_right, "lon", 1)
    next_mid = passed_along(mid_left, "lon", -1)
    prev_mid = passed_along(mid_right, "lon", 1)
    bias = (bias_left, bias_of(inputs, 1))
    last_out, below_out = attend(
        (
            (last_left, None, 0), (below_left, None, 0), (last_right, None, 0), (below_right, None, 0),
            (next_last, None, 0), (next_below, None, 0), (prev_last, None, 0), (prev_below, None, 0),
        ),
        order, w_qkv, w_proj, bias, 1,
    )
    bias, below_out = lax.optimization_barrier((bias, below_out))
    mid_a, mid_b = attend(
        [(array, 1, piece) for array in (mid_left, mid_right, next_mid, prev_mid) for piece in range(2)],
        order, w_qkv, w_proj, bias, 0,
    )
    first_out = passed_along(below_out, "lat", 1)
    merged = feed(tok, first_out, mid_a, mid_b, last_out, w_up, w_down, w_merge)
    return jnp.transpose(merged, (0, 3, 1, 2, 4))


def solution(mesh):
    in_specs = (
        P(None, None, "lat", "lon", None),
        P(),
        P(),
        P(),
        P(),
        P(),
        P("lat", None, None, None),
        P(),
        P("lat", None, None),
    )
    out_specs = P(None, None, "lat", "lon", None)
    return jax.shard_map(
        on_device, mesh=mesh, in_specs=in_specs, out_specs=out_specs, check_vma=False
    )
```

```python
import jax
import jax.numpy as jnp
import numpy as np
from jax import lax
from jax.experimental import pallas as pl
from jax.experimental.pallas import tpu as pltpu
from jax.sharding import PartitionSpec as P

HEADS = 12
HEAD_DIM = 32
C = 384
FFN = 1536
ZL = 8
ZW = 4
HALF = 72
SLOTS = 144
LANES = 256
CELLS = 288
PIECE = 144
LOG2E = 1.4426950408889634
BF = jnp.bfloat16
F32 = jnp.float32


def passed_along(block, axis, distance):
    devices = range(lax.axis_size(axis))
    route = [((i - distance) % len(devices), i) for i in devices]
    return lax.ppermute(block, axis, route)


def window_order():
    one_hot = np.zeros((CELLS, CELLS), np.float32)
    for zw in range(ZW):
        for z in range(2):
            for r in range(6):
                for c in range(6):
                    one_hot[zw * HALF + z * 36 + r * 6 + c, (r * 6 + c) * ZL + (2 * zw + 1 + z) % ZL] = 1.0
    return one_hot


def normalized(x):
    width = x.shape[-1]
    center = x - jnp.sum(x, axis=-1, keepdims=True) * (1.0 / width)
    spread = jnp.sum(center * center, axis=-1, keepdims=True) * (1.0 / width)
    return center * lax.rsqrt(spread + 1e-05)


def dot(a, b):
    return jnp.dot(a, b, preferred_element_type=F32)


def full(shape):
    return pl.BlockSpec(shape, lambda *i: (0,) * len(shape))


ROWS_AT_ONCE = 8
STEPS = SLOTS // ROWS_AT_ONCE
TYPE_HEADS = 96
PITCH = 97
TABLE = 3328
FORWARD = 6
PICKS = 4


def slot_order():
    return np.arange(SLOTS, dtype=np.int32).reshape(12, 2, 6).transpose(1, 0, 2).reshape(-1)


def gather_kernel(
    index_ref, tok_ref, table_ref, region_ref, region_col_ref,
    out_ref, mid_left, mid_right, last_left, last_right, below_left, below_right,
    next_mid, prev_mid, next_last, prev_last, next_below, prev_below,
    rows, picked, left, right, mids, firsts, lasts, send_sems, recv_sems, local_sems,
):
    step = pl.program_id(0)

    def neighbour(axis, distance):
        size = lax.axis_size(axis)
        return {axis: lax.rem(lax.axis_index(axis) + distance + size, size)}

    def remote(n, source, target, axis, distance):
        return pltpu.make_async_remote_copy(
            src_ref=source,
            dst_ref=target,
            send_sem=send_sems.at[n],
            recv_sem=recv_sems.at[n],
            device_id=neighbour(axis, distance),
            device_id_type=pl.DeviceIdType.MESH,
        )

    routes = (
        (firsts.at[0], below_left, "lat", -1),
        (firsts.at[1], below_right, "lat", -1),
        (lasts.at[0], next_last, "lon", -1),
        (lasts.at[1], prev_last, "lon", 1),
        (mids.at[0], next_mid, "lon", -1),
        (mids.at[1], prev_mid, "lon", 1),
        (below_left, next_below, "lon", -1),
        (below_right, prev_below, "lon", 1),
    )

    def block(n):
        return remote(n, *routes[n])

    def local():
        pairs = (
            (mids.at[0], mid_left), (mids.at[1], mid_right), (lasts.at[0], last_left), (lasts.at[1], last_right)
        )
        return [pltpu.make_async_copy(a, b, local_sems.at[n]) for n, (a, b) in enumerate(pairs)]

    @pl.when(step == 0)
    def _():
        barrier = pltpu.get_barrier_semaphore()
        for axis in ("lat", "lon"):
            for distance in (-1, 1):
                pl.semaphore_signal(
                    barrier, inc=1, device_id=neighbour(axis, distance), device_id_type=pl.DeviceIdType.MESH
                )
        for piece, blocks in ((0, (firsts,)), (3, (lasts,)), (1, (mids, 0)), (2, (mids, 1))):
            for b in range(tok_ref.shape[0]):
                x = normalized(tok_ref[b, 3 * piece : 3 * piece + 3].astype(F32))
                for side in range(2):
                    part = x[:, 6 * side : 6 * side + 6].reshape(PIECE, C).astype(BF)
                    if len(blocks) == 1:
                        blocks[0][side, b] = part
                    else:
                        blocks[0][side, b, blocks[1]] = part
            if piece == 0:
                pl.semaphore_wait(barrier, 4)
                block(0).start()
                block(1).start()
            elif piece == 3:
                block(2).start()
                block(3).start()
        block(4).start()
        block(5).start()
        for copy in local():
            copy.start()
        for c in range(TABLE // 128):
            rows[128 * c : 128 * (c + 1), :] = table_ref[:, 128 * c : 128 * (c + 1)].T

    @pl.when(step == FORWARD)
    def _():
        for n in range(2):
            block(n).wait_recv()
            block(6 + n).start()

    def pick(turn, carry):
        for j in range(PICKS):
            row = step * ROWS_AT_ONCE + turn * (PICKS // 2) + j // 2
            side, place = row // HALF, row % HALF
            start = ((place // 6) * 12 + side * 6 + place % 6) * SLOTS + j % 2 * 6
            base = pl.multiple_of(turn * (PICKS * HALF) + j * HALF, 8)
            for k in range(HALF):
                picked[pl.ds(base + k, 1), :] = rows[pl.ds(index_ref[start + k // 6 * 12 + k % 6], 1), :]
        return carry

    lax.fori_loop(0, ROWS_AT_ONCE * 2 // PICKS, pick, 0)
    for s in range(ROWS_AT_ONCE):
        left[PITCH * s : PITCH * s + TYPE_HEADS, :] = picked[SLOTS * s : SLOTS * s + 128, :].T[:TYPE_HEADS]
        right[PITCH * s : PITCH * s + TYPE_HEADS, :16] = picked[SLOTS * s + 128 : SLOTS * (s + 1), :].T[:TYPE_HEADS]
    for lw in range(2):
        for zw in range(ZW):
            kind = lw * ZW + zw
            same = region_col_ref[:, kind : kind + 1] == region_ref[kind : kind + 1, :]
            for h in range(HEADS):
                source = (lw * HEADS + h) * ZW + zw
                place = kind * HEADS + h
                out_ref[0, place, :, :128] = jnp.where(
                    same[:, :128], left[pl.ds(source, ROWS_AT_ONCE, stride=PITCH), :] * LOG2E, -1e9
                )
                out_ref[0, place, :, 128:] = jnp.where(
                    same[:, 128:], right[pl.ds(source, ROWS_AT_ONCE, stride=PITCH), :] * LOG2E, -1e9
                )

    @pl.when(step == STEPS - 1)
    def _():
        for n in range(8):
            block(n).wait_send()
            if n >= 2:
                block(n).wait_recv()
        for copy in local():
            copy.wait()


def gather(tok, earth_bias, position_index, region_ids):
    batch = tok.shape[0]
    index = position_index.reshape(-1)
    table = jnp.transpose(earth_bias, (0, 3, 1, 2)).reshape(TYPE_HEADS, -1)
    table = jnp.pad(table, ((0, 128 - TYPE_HEADS), (0, TABLE - table.shape[1])))
    region = region_ids.reshape(2 * ZW, SLOTS)[:, slot_order()]
    region_row = jnp.pad(region, ((0, 0), (0, LANES - SLOTS)), constant_values=-1)
    two, one = jax.ShapeDtypeStruct((batch, 2, PIECE, C), BF), jax.ShapeDtypeStruct((batch, PIECE, C), BF)
    anywhere = pl.BlockSpec(memory_space=pl.ANY)
    return pl.pallas_call(
        gather_kernel,
        grid=(STEPS,),
        in_specs=[
            pl.BlockSpec(memory_space=pltpu.SMEM),
            full(tok.shape),
            full((128, TABLE)),
            full((2 * ZW, LANES)),
            pl.BlockSpec((ROWS_AT_ONCE, 2 * ZW), lambda i: (i, 0)),
        ],
        out_specs=[pl.BlockSpec((1, TYPE_HEADS, ROWS_AT_ONCE, LANES), lambda i: (i, 0, 0, 0))] + [anywhere] * 12,
        out_shape=[jax.ShapeDtypeStruct((STEPS, TYPE_HEADS, ROWS_AT_ONCE, LANES), F32)]
        + [two, two, one, one, one, one, two, two, one, one, one, one],
        scratch_shapes=[
            pltpu.VMEM((TABLE, 128), F32),
            pltpu.VMEM((ROWS_AT_ONCE * SLOTS, 128), F32),
            pltpu.VMEM((ROWS_AT_ONCE * PITCH, 128), F32),
            pltpu.VMEM((ROWS_AT_ONCE * PITCH, 128), F32),
            pltpu.VMEM((2, batch, 2, PIECE, C), BF),
            pltpu.VMEM((2, batch, PIECE, C), BF),
            pltpu.VMEM((2, batch, PIECE, C), BF),
            pltpu.SemaphoreType.DMA((8,)),
            pltpu.SemaphoreType.DMA((8,)),
            pltpu.SemaphoreType.DMA((4,)),
        ],
        cost_estimate=pl.CostEstimate(flops=20_000_000, bytes_accessed=100_000_000, transcendentals=0),
        compiler_params=pltpu.CompilerParams(
            collective_id=0, has_side_effects=True, vmem_limit_bytes=60 << 20
        ),
        name="gather",
    )(index, tok, table, region_row, region.T)


def attend_kernel(
    lower_a, lower_b, upper_a, upper_b, right_a, right_b, left_a, left_b, order_ref, back_ref, w_qkv_ref, w_proj_ref, *rest
):
    bias_refs, (out_a, out_b, own_scr, halo_scr, ctx_scr) = rest[:2], rest[2:]
    order = order_ref[...]

    def windows(top, bottom):
        return dot(order, jnp.concatenate([top, bottom], axis=0)).astype(BF)

    own = jnp.concatenate([windows(upper_a[0], upper_b[0]), windows(lower_a[0], lower_b[0])], axis=0)
    own_scr[...] = dot(own, w_qkv_ref[...])
    halo = jnp.concatenate([windows(right_a[0], right_b[0]), windows(left_a[0], left_b[0])], axis=0)
    halo_scr[...] = dot(halo, w_qkv_ref[:, C:])
    lane_head = lax.broadcasted_iota(jnp.int32, (1, 128), 1) // HEAD_DIM
    masks = [lane_head == h for h in range(4)]
    ones = jnp.ones((SLOTS, 128), BF)

    for zw in range(ZW):
        for side in range(2):
            rows = slice(side * CELLS + zw * HALF, side * CELLS + (zw + 1) * HALF)
            for g in range(3):
                lanes = slice(128 * g, 128 * g + 128)
                klanes = slice(C + 128 * g, C + 128 * g + 128)
                vlanes = slice(2 * C + 128 * g, 2 * C + 128 * g + 128)
                q = own_scr[rows, lanes] * (HEAD_DIM ** (-0.5) * LOG2E)
                stacked = jnp.concatenate([jnp.where(m, q, 0.0) for m in masks], axis=0).astype(BF)
                k = [own_scr[rows, klanes], halo_scr[rows, lanes]]
                v = [own_scr[rows, vlanes], halo_scr[rows, klanes]]
                if side == 1:
                    k, v = k[::-1], v[::-1]
                keys = jnp.concatenate(k, axis=0).astype(BF)
                values = jnp.concatenate([jnp.concatenate(v, axis=0).astype(BF), ones], axis=1)
                scores = lax.dot_general(stacked, keys, (((1,), (1,)), ((), ())), preferred_element_type=F32)
                bias = jnp.swapaxes(bias_refs[side][:, zw * HEADS + 4 * g : zw * HEADS + 4 * g + 4, :, :SLOTS], 0, 1)
                scores = scores + bias.reshape(4 * HALF, SLOTS)
                raised = jnp.exp2(scores - jnp.max(scores, axis=-1, keepdims=True)).astype(BF)
                both = dot(raised, values)
                top, total = both[:HALF, :128], both[:HALF, 128:]
                for h in range(1, 4):
                    top = jnp.where(masks[h], both[h * HALF : (h + 1) * HALF, :128], top)
                    total = jnp.where(masks[h], both[h * HALF : (h + 1) * HALF, 128:], total)
                ctx_scr[rows, lanes] = top / total
    back = back_ref[...]
    for side in range(2):
        natural = dot(back, ctx_scr[CELLS * side : CELLS * (side + 1), :].astype(BF)).astype(BF)
        result = dot(natural, w_proj_ref[...]).astype(BF)
        out_a[1 - side, 0] = result[:PIECE]
        out_b[1 - side, 0] = result[PIECE:]


def attend(streams, order, w_qkv, w_proj, bias, lw):
    batch = streams[-1][0].shape[0]
    arrays, specs = [], []
    for array, dim, index in streams:
        arrays.append(array)
        if dim is None:
            specs.append(pl.BlockSpec((1, PIECE, C), lambda b: (b, 0, 0)))
        elif dim == 0:
            specs.append(pl.BlockSpec((None, 1, PIECE, C), lambda b, i=index: (i, b, 0, 0)))
        else:
            specs.append(pl.BlockSpec((1, None, PIECE, C), lambda b, i=index: (b, i, 0, 0)))
    out = jax.ShapeDtypeStruct((2, batch, PIECE, C), BF)
    out_spec = pl.BlockSpec((2, 1, PIECE, C), lambda b: (0, b, 0, 0))
    return pl.pallas_call(
        attend_kernel,
        grid=(batch,),
        in_specs=specs
        + [
            full((CELLS, CELLS)),
            full((CELLS, CELLS)),
            full((C, 3 * C)),
            full((C, C)),
            pl.BlockSpec((STEPS // 2, ZW * HEADS, ROWS_AT_ONCE, LANES), lambda b: (0, lw, 0, 0)),
            pl.BlockSpec((STEPS // 2, ZW * HEADS, ROWS_AT_ONCE, LANES), lambda b: (1, lw, 0, 0)),
        ],
        out_specs=[out_spec, out_spec],
        out_shape=[out, out],
        scratch_shapes=[
            pltpu.VMEM((2 * CELLS, 3 * C), F32),
            pltpu.VMEM((2 * CELLS, 2 * C), F32),
            pltpu.VMEM((2 * CELLS, C), F32),
        ],
        cost_estimate=pl.CostEstimate(flops=20_000_000_000, bytes_accessed=16_000_000, transcendentals=4_000_000),
        compiler_params=pltpu.CompilerParams(vmem_limit_bytes=60 << 20),
        name="attend",
    )(*arrays, jnp.asarray(order, BF), jnp.asarray(order.T, BF), w_qkv, w_proj, bias, bias)


CHUNK = 768


def feed_kernel(tok_ref, first_ref, mid_a, mid_b, last_ref, w_up_ref, w_down_ref, w_merge_ref, out_ref, hidden_scr):
    for piece, ref in enumerate((first_ref, mid_a, mid_b, last_ref)):
        for side in range(2):
            rows, cols = slice(3 * piece, 3 * piece + 3), slice(6 * side, 6 * side + 6)
            tok = tok_ref[0, rows, cols].astype(F32)
            attended = ref[side, 0].astype(F32).reshape(3, 6, ZL, C)
            hidden_scr[rows, cols] = (tok + attended).astype(BF).astype(F32)

    hidden = hidden_scr[...].reshape(12 * 12 * ZL, C)
    normed = normalized(hidden).astype(BF)
    block = hidden
    for f in range(0, FFN, CHUNK):
        up = dot(normed, w_up_ref[:, f : f + CHUNK])
        inner = (0.5 * up * (1.0 + lax.erf(up * 0.7071067811865476))).astype(BF)
        block = block + dot(inner, w_down_ref[f : f + CHUNK])
    block = block.astype(BF).astype(F32).reshape(6, 2, 6, 2, ZL, C)
    grouped = jnp.concatenate([block[:, p // 2, :, p % 2] for p in range(4)], axis=-1)
    grouped = normalized(grouped.reshape(36 * ZL, 4 * C)).astype(BF)
    out_ref[0] = dot(grouped, w_merge_ref[...]).reshape(6, 6, ZL, 2 * C).astype(BF)


def feed(tok, first, mid_a, mid_b, last, w_up, w_down, w_merge):
    batch = tok.shape[0]
    piece = pl.BlockSpec((2, 1, PIECE, C), lambda b: (0, b, 0, 0))
    return pl.pallas_call(
        feed_kernel,
        grid=(batch,),
        in_specs=[
            pl.BlockSpec((1, 12, 12, ZL, C), lambda b: (b, 0, 0, 0, 0)),
            piece,
            piece,
            piece,
            piece,
            full((C, FFN)),
            full((FFN, C)),
            full((4 * C, 2 * C)),
        ],
        out_specs=pl.BlockSpec((1, 6, 6, ZL, 2 * C), lambda b: (b, 0, 0, 0, 0)),
        out_shape=jax.ShapeDtypeStruct((batch, 6, 6, ZL, 2 * C), BF),
        scratch_shapes=[pltpu.VMEM((12, 12, ZL, C), F32)],
        cost_estimate=pl.CostEstimate(flops=14_000_000_000, bytes_accessed=14_000_000, transcendentals=7_000_000),
        compiler_params=pltpu.CompilerParams(vmem_limit_bytes=60 << 20),
        name="feed",
    )(tok, first, mid_a, mid_b, last, w_up, w_down, w_merge)


def on_device(tokens, w_qkv, w_proj, w_up, w_down, w_merge, earth_bias, position_index, region_ids):
    tok = jnp.transpose(tokens, (0, 2, 3, 1, 4))
    order = window_order()
    (
        bias, mid_left, mid_right, last_left, last_right, below_left, below_right,
        next_mid, prev_mid, next_last, prev_last, next_below, prev_below,
    ) = gather(tok, earth_bias, position_index, region_ids)
    last_out, below_out = attend(
        [
            (array, None, 0)
            for array in (
                last_left, below_left, last_right, below_right, next_last, next_below, prev_last, prev_below
            )
        ],
        order, w_qkv, w_proj, bias, 1,
    )
    bias, below_out = lax.optimization_barrier((bias, below_out))
    mid_a, mid_b = attend(
        [(array, 1, piece) for array in (mid_left, mid_right, next_mid, prev_mid) for piece in range(2)],
        order, w_qkv, w_proj, bias, 0,
    )
    first_out = passed_along(below_out, "lat", 1)
    merged = feed(tok, first_out, mid_a, mid_b, last_out, w_up, w_down, w_merge)
    return jnp.transpose(merged, (0, 3, 1, 2, 4))


def solution(mesh):
    in_specs = (
        P(None, None, "lat", "lon", None),
        P(),
        P(),
        P(),
        P(),
        P(),
        P("lat", None, None, None),
        P(),
        P("lat", None, None),
    )
    out_specs = P(None, None, "lat", "lon", None)
    return jax.shard_map(
        on_device, mesh=mesh, in_specs=in_specs, out_specs=out_specs, check_vma=False
    )
```

```python
import jax
import jax.numpy as jnp
import numpy as np
from jax import lax
from jax.experimental import pallas as pl
from jax.experimental.pallas import tpu as pltpu
from jax.sharding import PartitionSpec as P

HEADS = 12
HEAD_DIM = 32
C = 384
FFN = 1536
ZL = 8
ZW = 4
HALF = 72
SLOTS = 144
LANES = 256
CELLS = 288
PIECE = 144
LOG2E = 1.4426950408889634
BF = jnp.bfloat16
F32 = jnp.float32


def passed_along(block, axis, distance):
    devices = range(lax.axis_size(axis))
    route = [((i - distance) % len(devices), i) for i in devices]
    return lax.ppermute(block, axis, route)


def window_order():
    one_hot = np.zeros((CELLS, CELLS), np.float32)
    for zw in range(ZW):
        for z in range(2):
            for r in range(6):
                for c in range(6):
                    one_hot[zw * HALF + z * 36 + r * 6 + c, (r * 6 + c) * ZL + (2 * zw + 1 + z) % ZL] = 1.0
    return one_hot


def normalized(x):
    width = x.shape[-1]
    center = x - jnp.sum(x, axis=-1, keepdims=True) * (1.0 / width)
    spread = jnp.sum(center * center, axis=-1, keepdims=True) * (1.0 / width)
    return center * lax.rsqrt(spread + 1e-05)


def dot(a, b):
    return jnp.dot(a, b, preferred_element_type=F32)


def neighbour(axis, distance):
    size = lax.axis_size(axis)
    return {axis: lax.rem(lax.axis_index(axis) + distance + size, size)}


def remote(source, target, send_sem, recv_sem, axis, distance):
    return pltpu.make_async_remote_copy(
        src_ref=source,
        dst_ref=target,
        send_sem=send_sem,
        recv_sem=recv_sem,
        device_id=neighbour(axis, distance),
        device_id_type=pl.DeviceIdType.MESH,
    )


def greet(axes):
    barrier = pltpu.get_barrier_semaphore()
    for axis in axes:
        for distance in (-1, 1):
            pl.semaphore_signal(
                barrier, inc=1, device_id=neighbour(axis, distance), device_id_type=pl.DeviceIdType.MESH
            )


def greeted(axes):
    pl.semaphore_wait(pltpu.get_barrier_semaphore(), 2 * len(axes))


def full(shape):
    return pl.BlockSpec(shape, lambda *i: (0,) * len(shape))


ROWS_AT_ONCE = 8
STEPS = SLOTS // ROWS_AT_ONCE
TYPE_HEADS = 96
PITCH = 97
TABLE = 3312
FORWARD = 8
PICKS = 4


def slot_order():
    return np.arange(SLOTS, dtype=np.int32).reshape(12, 2, 6).transpose(1, 0, 2).reshape(-1)


def gather_kernel(
    index_ref, tok_ref, table_ref, labels_ref, slots_ref,
    out_ref, mid_left, mid_right, last_left, last_right, below_left, below_right,
    next_last, prev_last, next_below, prev_below,
    rows, picked, left, right, region_ref, region_col_ref, mids, firsts, lasts, send_sems, recv_sems, local_sems,
):
    step = pl.program_id(0)

    routes = (
        (firsts.at[0], below_left, "lat", -1),
        (firsts.at[1], below_right, "lat", -1),
        (lasts.at[0], next_last, "lon", -1),
        (lasts.at[1], prev_last, "lon", 1),
        (below_left, next_below, "lon", -1),
        (below_right, prev_below, "lon", 1),
    )

    def block(n):
        source, target, axis, distance = routes[n]
        return remote(source, target, send_sems.at[n], recv_sems.at[n], axis, distance)

    def local():
        pairs = (
            (mids.at[0], mid_left), (mids.at[1], mid_right), (lasts.at[0], last_left), (lasts.at[1], last_right)
        )
        return [pltpu.make_async_copy(a, b, local_sems.at[n]) for n, (a, b) in enumerate(pairs)]

    @pl.when(step == 0)
    def _():
        greet(("lat", "lon"))
        for piece, blocks in ((0, (firsts,)), (3, (lasts,)), (1, (mids, 0)), (2, (mids, 1))):
            for b in range(tok_ref.shape[0]):
                x = normalized(tok_ref[b, 3 * piece : 3 * piece + 3].astype(F32))
                for side in range(2):
                    part = x[:, 6 * side : 6 * side + 6].reshape(PIECE, C).astype(BF)
                    if len(blocks) == 1:
                        blocks[0][side, b] = part
                    else:
                        blocks[0][side, b, blocks[1]] = part
            if piece == 0:
                greeted(("lat", "lon"))
                block(0).start()
                block(1).start()
            elif piece == 3:
                block(2).start()
                block(3).start()
        for copy in local():
            copy.start()
        for c in range(0, TABLE, 128):
            width = min(128, TABLE - c)
            some = table_ref[:, :, :, c : c + width].reshape(TYPE_HEADS, width)
            rows[c : c + width, :TYPE_HEADS] = some.T
        labels = dot((labels_ref[...] + 1).astype(F32).astype(BF), slots_ref[...])
        region_ref[...] = labels
        region_col_ref[...] = labels.T

    @pl.when(step == FORWARD)
    def _():
        for n in range(2):
            block(n).wait_recv()
            block(4 + n).start()

    def pick(turn, carry):
        for j in range(PICKS):
            row = step * ROWS_AT_ONCE + turn * (PICKS // 2) + j // 2
            side, place = row // HALF, row % HALF
            slot = (place // 6) * 12 + side * 6 + place % 6
            base = pl.multiple_of(turn * (PICKS * HALF) + j * HALF, 8)
            for k in range(HALF):
                picked[pl.ds(base + k, 1), :] = rows[pl.ds(index_ref[slot, j % 2 * 6 + k // 6 * 12 + k % 6], 1), :]
        return carry

    lax.fori_loop(0, ROWS_AT_ONCE * 2 // PICKS, pick, 0)
    for s in range(ROWS_AT_ONCE):
        left[PITCH * s : PITCH * s + TYPE_HEADS, :] = picked[SLOTS * s : SLOTS * s + 128, :].T[:TYPE_HEADS]
        right[PITCH * s : PITCH * s + TYPE_HEADS, :16] = picked[SLOTS * s + 128 : SLOTS * (s + 1), :].T[:TYPE_HEADS]
    for lw in range(2):
        for zw in range(ZW):
            kind = lw * ZW + zw
            same = region_col_ref[pl.ds(pl.multiple_of(step * ROWS_AT_ONCE, 8), ROWS_AT_ONCE), kind : kind + 1] == region_ref[kind : kind + 1, :]
            for h in range(HEADS):
                source = (lw * HEADS + h) * ZW + zw
                place = kind * HEADS + h
                out_ref[0, place, :, :128] = jnp.where(
                    same[:, :128], left[pl.ds(source, ROWS_AT_ONCE, stride=PITCH), :] * LOG2E, -1e9
                )
                out_ref[0, place, :, 128:] = jnp.where(
                    same[:, 128:], right[pl.ds(source, ROWS_AT_ONCE, stride=PITCH), :] * LOG2E, -1e9
                )

    @pl.when(step == STEPS - 1)
    def _():
        for n in range(6):
            block(n).wait_send()
            if n >= 2:
                block(n).wait_recv()
        for copy in local():
            copy.wait()


def gather(tok, earth_bias, position_index, region_ids):
    batch = tok.shape[0]
    table = jnp.transpose(earth_bias, (0, 3, 1, 2))
    slots = np.zeros((SLOTS, LANES), np.float32)
    slots[slot_order(), np.arange(SLOTS)] = 1.0
    two, one = jax.ShapeDtypeStruct((batch, 2, PIECE, C), BF), jax.ShapeDtypeStruct((batch, PIECE, C), BF)
    anywhere = pl.BlockSpec(memory_space=pl.ANY)
    return pl.pallas_call(
        gather_kernel,
        grid=(STEPS,),
        in_specs=[
            pl.BlockSpec(memory_space=pltpu.SMEM),
            full(tok.shape),
            full(table.shape),
            full((2 * ZW, SLOTS)),
            full((SLOTS, LANES)),
        ],
        out_specs=[pl.BlockSpec((1, TYPE_HEADS, ROWS_AT_ONCE, LANES), lambda i: (i, 0, 0, 0))] + [anywhere] * 10,
        out_shape=[jax.ShapeDtypeStruct((STEPS, TYPE_HEADS, ROWS_AT_ONCE, LANES), F32)]
        + [two, two] + [one] * 8,
        scratch_shapes=[
            pltpu.VMEM((TABLE, 128), F32),
            pltpu.VMEM((ROWS_AT_ONCE * SLOTS, 128), F32),
            pltpu.VMEM((ROWS_AT_ONCE * PITCH, 128), F32),
            pltpu.VMEM((ROWS_AT_ONCE * PITCH, 128), F32),
            pltpu.VMEM((2 * ZW, LANES), F32),
            pltpu.VMEM((LANES, 2 * ZW), F32),
            pltpu.VMEM((2, batch, 2, PIECE, C), BF),
            pltpu.VMEM((2, batch, PIECE, C), BF),
            pltpu.VMEM((2, batch, PIECE, C), BF),
            pltpu.SemaphoreType.DMA((6,)),
            pltpu.SemaphoreType.DMA((6,)),
            pltpu.SemaphoreType.DMA((4,)),
        ],
        cost_estimate=pl.CostEstimate(flops=20_000_000, bytes_accessed=100_000_000, transcendentals=0),
        compiler_params=pltpu.CompilerParams(
            collective_id=0, has_side_effects=True, vmem_limit_bytes=60 << 20
        ),
        name="gather",
    )(position_index, tok, table, region_ids.reshape(2 * ZW, SLOTS), jnp.asarray(slots, BF))


def attend_kernel(
    lower_a, lower_b, upper_a, upper_b, right_a, right_b, left_a, left_b, order_ref, back_ref, w_qkv_ref, w_proj_ref, *rest
):
    bias_refs, rest = rest[:2], rest[2:]
    if len(rest) > 5:
        mid_left, mid_right, out_a, out_b, next_mid, prev_mid, own_scr, halo_scr, ctx_scr, send_sems, recv_sems = rest

        def blocks():
            return (
                remote(mid_left, next_mid, send_sems.at[0], recv_sems.at[0], "lon", -1),
                remote(mid_right, prev_mid, send_sems.at[1], recv_sems.at[1], "lon", 1),
            )

        @pl.when(pl.program_id(0) == 0)
        def _():
            greet(("lon",))
            greeted(("lon",))
            for block in blocks():
                block.start()
    else:
        blocks = None
        out_a, out_b, own_scr, halo_scr, ctx_scr = rest
    order = order_ref[...]

    def windows(top, bottom):
        return dot(order, jnp.concatenate([top, bottom], axis=0)).astype(BF)

    own = jnp.concatenate([windows(upper_a[0], upper_b[0]), windows(lower_a[0], lower_b[0])], axis=0)
    own_scr[...] = dot(own, w_qkv_ref[...])
    halo = jnp.concatenate([windows(right_a[0], right_b[0]), windows(left_a[0], left_b[0])], axis=0)
    halo_scr[...] = dot(halo, w_qkv_ref[:, C:])
    lane_head = lax.broadcasted_iota(jnp.int32, (1, 128), 1) // HEAD_DIM
    masks = [lane_head == h for h in range(4)]
    ones = jnp.ones((SLOTS, 128), BF)

    for zw in range(ZW):
        for side in range(2):
            rows = slice(side * CELLS + zw * HALF, side * CELLS + (zw + 1) * HALF)
            for g in range(3):
                lanes = slice(128 * g, 128 * g + 128)
                klanes = slice(C + 128 * g, C + 128 * g + 128)
                vlanes = slice(2 * C + 128 * g, 2 * C + 128 * g + 128)
                q = own_scr[rows, lanes] * (HEAD_DIM ** (-0.5) * LOG2E)
                stacked = jnp.concatenate([jnp.where(m, q, 0.0) for m in masks], axis=0).astype(BF)
                k = [own_scr[rows, klanes], halo_scr[rows, lanes]]
                v = [own_scr[rows, vlanes], halo_scr[rows, klanes]]
                if side == 1:
                    k, v = k[::-1], v[::-1]
                keys = jnp.concatenate(k, axis=0).astype(BF)
                values = jnp.concatenate([jnp.concatenate(v, axis=0).astype(BF), ones], axis=1)
                scores = lax.dot_general(stacked, keys, (((1,), (1,)), ((), ())), preferred_element_type=F32)
                bias = jnp.swapaxes(bias_refs[side][:, zw * HEADS + 4 * g : zw * HEADS + 4 * g + 4, :, :SLOTS], 0, 1)
                scores = scores + bias.reshape(4 * HALF, SLOTS)
                raised = jnp.exp2(scores - jnp.max(scores, axis=-1, keepdims=True)).astype(BF)
                both = dot(raised, values)
                top, total = both[:HALF, :128], both[:HALF, 128:]
                for h in range(1, 4):
                    top = jnp.where(masks[h], both[h * HALF : (h + 1) * HALF, :128], top)
                    total = jnp.where(masks[h], both[h * HALF : (h + 1) * HALF, 128:], total)
                ctx_scr[rows, lanes] = top / total
    back = back_ref[...]
    for side in range(2):
        natural = dot(back, ctx_scr[CELLS * side : CELLS * (side + 1), :].astype(BF)).astype(BF)
        result = dot(natural, w_proj_ref[...]).astype(BF)
        out_a[1 - side, 0] = result[:PIECE]
        out_b[1 - side, 0] = result[PIECE:]
    if blocks is not None:

        @pl.when(pl.program_id(0) == pl.num_programs(0) - 1)
        def _():
            for block in blocks():
                block.wait()


def attend(streams, order, w_qkv, w_proj, bias, lw, travelling=()):
    batch = streams[-1][0].shape[0]
    arrays, specs = [], []
    for array, dim, index in streams:
        arrays.append(array)
        if dim is None:
            specs.append(pl.BlockSpec((1, PIECE, C), lambda b: (b, 0, 0)))
        elif dim == 0:
            specs.append(pl.BlockSpec((None, 1, PIECE, C), lambda b, i=index: (i, b, 0, 0)))
        else:
            specs.append(pl.BlockSpec((1, None, PIECE, C), lambda b, i=index: (b, i, 0, 0)))
    anywhere = [pl.BlockSpec(memory_space=pl.ANY)] * len(travelling)
    sems = [pltpu.SemaphoreType.DMA((2,))] * len(travelling)
    remote_params = dict(collective_id=1, has_side_effects=True) if travelling else {}
    out = jax.ShapeDtypeStruct((2, batch, PIECE, C), BF)
    out_spec = pl.BlockSpec((2, 1, PIECE, C), lambda b: (0, b, 0, 0))
    return pl.pallas_call(
        attend_kernel,
        grid=(batch,),
        in_specs=specs
        + [
            full((CELLS, CELLS)),
            full((CELLS, CELLS)),
            full((C, 3 * C)),
            full((C, C)),
            pl.BlockSpec((STEPS // 2, ZW * HEADS, ROWS_AT_ONCE, LANES), lambda b: (0, lw, 0, 0)),
            pl.BlockSpec((STEPS // 2, ZW * HEADS, ROWS_AT_ONCE, LANES), lambda b: (1, lw, 0, 0)),
        ]
        + anywhere,
        out_specs=[out_spec, out_spec] + anywhere,
        out_shape=[out, out] + [jax.ShapeDtypeStruct(array.shape, BF) for array in travelling],
        scratch_shapes=[
            pltpu.VMEM((2 * CELLS, 3 * C), F32),
            pltpu.VMEM((2 * CELLS, 2 * C), F32),
            pltpu.VMEM((2 * CELLS, C), F32),
        ]
        + sems,
        cost_estimate=pl.CostEstimate(flops=20_000_000_000, bytes_accessed=16_000_000, transcendentals=4_000_000),
        compiler_params=pltpu.CompilerParams(vmem_limit_bytes=60 << 20, **remote_params),
        name="attend",
    )(*arrays, jnp.asarray(order, BF), jnp.asarray(order.T, BF), w_qkv, w_proj, bias, bias, *travelling)


CHUNK = 768


def feed_kernel(tok_ref, first_ref, mid_a, mid_b, last_ref, w_up_ref, w_down_ref, w_merge_ref, out_ref, hidden_scr):
    for piece, ref in enumerate((first_ref, mid_a, mid_b, last_ref)):
        for side in range(2):
            rows, cols = slice(3 * piece, 3 * piece + 3), slice(6 * side, 6 * side + 6)
            tok = tok_ref[0, rows, cols].astype(F32)
            attended = ref[side, 0].astype(F32).reshape(3, 6, ZL, C)
            hidden_scr[rows, cols] = (tok + attended).astype(BF).astype(F32)

    hidden = hidden_scr[...].reshape(12 * 12 * ZL, C)
    normed = normalized(hidden).astype(BF)
    block = hidden
    for f in range(0, FFN, CHUNK):
        up = dot(normed, w_up_ref[:, f : f + CHUNK])
        inner = (0.5 * up * (1.0 + lax.erf(up * 0.7071067811865476))).astype(BF)
        block = block + dot(inner, w_down_ref[f : f + CHUNK])
    block = block.astype(BF).astype(F32).reshape(6, 2, 6, 2, ZL, C)
    grouped = jnp.concatenate([block[:, p // 2, :, p % 2] for p in range(4)], axis=-1)
    grouped = normalized(grouped.reshape(36 * ZL, 4 * C)).astype(BF)
    out_ref[0] = dot(grouped, w_merge_ref[...]).reshape(6, 6, ZL, 2 * C).astype(BF)


def feed(tok, first, mid_a, mid_b, last, w_up, w_down, w_merge):
    batch = tok.shape[0]
    piece = pl.BlockSpec((2, 1, PIECE, C), lambda b: (0, b, 0, 0))
    return pl.pallas_call(
        feed_kernel,
        grid=(batch,),
        in_specs=[
            pl.BlockSpec((1, 12, 12, ZL, C), lambda b: (b, 0, 0, 0, 0)),
            piece,
            piece,
            piece,
            piece,
            full((C, FFN)),
            full((FFN, C)),
            full((4 * C, 2 * C)),
        ],
        out_specs=pl.BlockSpec((1, 6, 6, ZL, 2 * C), lambda b: (b, 0, 0, 0, 0)),
        out_shape=jax.ShapeDtypeStruct((batch, 6, 6, ZL, 2 * C), BF),
        scratch_shapes=[pltpu.VMEM((12, 12, ZL, C), F32)],
        cost_estimate=pl.CostEstimate(flops=14_000_000_000, bytes_accessed=14_000_000, transcendentals=7_000_000),
        compiler_params=pltpu.CompilerParams(vmem_limit_bytes=60 << 20),
        name="feed",
    )(tok, first, mid_a, mid_b, last, w_up, w_down, w_merge)


def on_device(tokens, w_qkv, w_proj, w_up, w_down, w_merge, earth_bias, position_index, region_ids):
    tok = jnp.transpose(tokens, (0, 2, 3, 1, 4))
    order = window_order()
    (
        bias, mid_left, mid_right, last_left, last_right, below_left, below_right,
        next_last, prev_last, next_below, prev_below,
    ) = gather(tok, earth_bias, position_index, region_ids)
    last_out, below_out, next_mid, prev_mid = attend(
        [
            (array, None, 0)
            for array in (
                last_left, below_left, last_right, below_right, next_last, next_below, prev_last, prev_below
            )
        ],
        order, w_qkv, w_proj, bias, 1, (mid_left, mid_right),
    )
    mid_a, mid_b = attend(
        [(array, 1, piece) for array in (mid_left, mid_right, next_mid, prev_mid) for piece in range(2)],
        order, w_qkv, w_proj, bias, 0,
    )
    first_out = passed_along(below_out, "lat", 1)
    merged = feed(tok, first_out, mid_a, mid_b, last_out, w_up, w_down, w_merge)
    return jnp.transpose(merged, (0, 3, 1, 2, 4))


def solution(mesh):
    in_specs = (
        P(None, None, "lat", "lon", None),
        P(),
        P(),
        P(),
        P(),
        P(),
        P("lat", None, None, None),
        P(),
        P("lat", None, None),
    )
    out_specs = P(None, None, "lat", "lon", None)
    return jax.shard_map(
        on_device, mesh=mesh, in_specs=in_specs, out_specs=out_specs, check_vma=False
    )
```

```python
import jax
import jax.numpy as jnp
import numpy as np
from jax import lax
from jax.experimental import pallas as pl
from jax.experimental.pallas import tpu as pltpu
from jax.sharding import PartitionSpec as P

HEADS = 12
HEAD_DIM = 32
C = 384
FFN = 1536
ZL = 8
ZW = 4
HALF = 72
SLOTS = 144
LANES = 256
CELLS = 288
PIECE = 144
LOG2E = 1.4426950408889634
BF = jnp.bfloat16
F32 = jnp.float32


def passed_along(block, axis, distance):
    devices = range(lax.axis_size(axis))
    route = [((i - distance) % len(devices), i) for i in devices]
    return lax.ppermute(block, axis, route)


def window_order():
    one_hot = np.zeros((CELLS, CELLS), np.float32)
    for zw in range(ZW):
        for z in range(2):
            for r in range(6):
                for c in range(6):
                    one_hot[zw * HALF + z * 36 + r * 6 + c, (r * 6 + c) * ZL + (2 * zw + 1 + z) % ZL] = 1.0
    return one_hot


def normalized(x):
    width = x.shape[-1]
    center = x - jnp.sum(x, axis=-1, keepdims=True) * (1.0 / width)
    spread = jnp.sum(center * center, axis=-1, keepdims=True) * (1.0 / width)
    return center * lax.rsqrt(spread + 1e-05)


def dot(a, b):
    return jnp.dot(a, b, preferred_element_type=F32)


def neighbour(axis, distance):
    size = lax.axis_size(axis)
    return {axis: lax.rem(lax.axis_index(axis) + distance + size, size)}


def remote(source, target, send_sem, recv_sem, axis, distance):
    return pltpu.make_async_remote_copy(
        src_ref=source,
        dst_ref=target,
        send_sem=send_sem,
        recv_sem=recv_sem,
        device_id=neighbour(axis, distance),
        device_id_type=pl.DeviceIdType.MESH,
    )


def greet(axes):
    barrier = pltpu.get_barrier_semaphore()
    for axis in axes:
        for distance in (-1, 1):
            pl.semaphore_signal(
                barrier, inc=1, device_id=neighbour(axis, distance), device_id_type=pl.DeviceIdType.MESH
            )


def greeted(axes):
    pl.semaphore_wait(pltpu.get_barrier_semaphore(), 2 * len(axes))


def full(shape):
    return pl.BlockSpec(shape, lambda *i: (0,) * len(shape))


ROWS_AT_ONCE = 8
STEPS = SLOTS // ROWS_AT_ONCE
TYPE_HEADS = 96
PITCH = 97
TABLE = 3312
ALONG = 4
FORWARD = 10
PICKS = 4


def slot_order():
    return np.arange(SLOTS, dtype=np.int32).reshape(12, 2, 6).transpose(1, 0, 2).reshape(-1)


def gather_kernel(
    index_ref, tok_ref, table_ref, labels_ref, slots_ref,
    out_ref, mid_left, mid_right, last_left, last_right, below_left, below_right,
    next_last, prev_last, next_below, prev_below,
    rows, picked, left, right, region_ref, region_col_ref, mids, firsts, lasts, send_sems, recv_sems, local_sems,
):
    step = pl.program_id(0)

    routes = (
        (firsts.at[0], below_left, "lat", -1),
        (firsts.at[1], below_right, "lat", -1),
        (lasts.at[0], next_last, "lon", -1),
        (lasts.at[1], prev_last, "lon", 1),
        (below_left, next_below, "lon", -1),
        (below_right, prev_below, "lon", 1),
    )

    def block(n):
        source, target, axis, distance = routes[n]
        return remote(source, target, send_sems.at[n], recv_sems.at[n], axis, distance)

    def local():
        pairs = (
            (mids.at[0], mid_left), (mids.at[1], mid_right), (lasts.at[0], last_left), (lasts.at[1], last_right)
        )
        return [pltpu.make_async_copy(a, b, local_sems.at[n]) for n, (a, b) in enumerate(pairs)]

    @pl.when(step == 0)
    def _():
        greet(("lat", "lon"))
        for piece, blocks in ((0, (firsts,)), (3, (lasts,)), (1, (mids, 0)), (2, (mids, 1))):
            for b in range(tok_ref.shape[0]):
                x = normalized(tok_ref[b, 3 * piece : 3 * piece + 3].astype(F32))
                for side in range(2):
                    part = x[:, 6 * side : 6 * side + 6].reshape(PIECE, C).astype(BF)
                    if len(blocks) == 1:
                        blocks[0][side, b] = part
                    else:
                        blocks[0][side, b, blocks[1]] = part
            if piece == 0:
                greeted(("lat", "lon"))
                block(0).start()
                block(1).start()
        for copy in local():
            copy.start()
        for c in range(0, TABLE, 128):
            width = min(128, TABLE - c)
            some = table_ref[:, :, :, c : c + width].reshape(TYPE_HEADS, width)
            rows[c : c + width, :TYPE_HEADS] = some.T
        labels = dot((labels_ref[...] + 1).astype(F32).astype(BF), slots_ref[...])
        region_ref[...] = labels
        region_col_ref[...] = labels.T

    @pl.when(step == ALONG)
    def _():
        block(2).start()
        block(3).start()

    @pl.when(step == FORWARD)
    def _():
        for n in range(2):
            block(n).wait_recv()
            block(4 + n).start()

    def pick(turn, carry):
        for j in range(PICKS):
            row = step * ROWS_AT_ONCE + turn * (PICKS // 2) + j // 2
            side, place = row // HALF, row % HALF
            slot = (place // 6) * 12 + side * 6 + place % 6
            base = pl.multiple_of(turn * (PICKS * HALF) + j * HALF, 8)
            for k in range(HALF):
                picked[pl.ds(base + k, 1), :] = rows[pl.ds(index_ref[slot, j % 2 * 6 + k // 6 * 12 + k % 6], 1), :]
        return carry

    lax.fori_loop(0, ROWS_AT_ONCE * 2 // PICKS, pick, 0)
    for s in range(ROWS_AT_ONCE):
        left[PITCH * s : PITCH * s + TYPE_HEADS, :] = picked[SLOTS * s : SLOTS * s + 128, :].T[:TYPE_HEADS]
        right[PITCH * s : PITCH * s + TYPE_HEADS, :16] = picked[SLOTS * s + 128 : SLOTS * (s + 1), :].T[:TYPE_HEADS]
    for lw in range(2):
        for zw in range(ZW):
            kind = lw * ZW + zw
            same = region_col_ref[pl.ds(pl.multiple_of(step * ROWS_AT_ONCE, 8), ROWS_AT_ONCE), kind : kind + 1] == region_ref[kind : kind + 1, :]
            for h in range(HEADS):
                source = (lw * HEADS + h) * ZW + zw
                place = kind * HEADS + h
                out_ref[0, place, :, :128] = jnp.where(
                    same[:, :128], left[pl.ds(source, ROWS_AT_ONCE, stride=PITCH), :] * LOG2E, -1e9
                )
                out_ref[0, place, :, 128:] = jnp.where(
                    same[:, 128:], right[pl.ds(source, ROWS_AT_ONCE, stride=PITCH), :] * LOG2E, -1e9
                )

    @pl.when(step == STEPS - 1)
    def _():
        for n in range(6):
            block(n).wait_send()
            if n >= 2:
                block(n).wait_recv()
        for copy in local():
            copy.wait()


def gather(tok, earth_bias, position_index, region_ids):
    batch = tok.shape[0]
    table = jnp.transpose(earth_bias, (0, 3, 1, 2))
    slots = np.zeros((SLOTS, LANES), np.float32)
    slots[slot_order(), np.arange(SLOTS)] = 1.0
    two, one = jax.ShapeDtypeStruct((batch, 2, PIECE, C), BF), jax.ShapeDtypeStruct((batch, PIECE, C), BF)
    anywhere = pl.BlockSpec(memory_space=pl.ANY)
    return pl.pallas_call(
        gather_kernel,
        grid=(STEPS,),
        in_specs=[
            pl.BlockSpec(memory_space=pltpu.SMEM),
            full(tok.shape),
            full(table.shape),
            full((2 * ZW, SLOTS)),
            full((SLOTS, LANES)),
        ],
        out_specs=[pl.BlockSpec((1, TYPE_HEADS, ROWS_AT_ONCE, LANES), lambda i: (i, 0, 0, 0))] + [anywhere] * 10,
        out_shape=[jax.ShapeDtypeStruct((STEPS, TYPE_HEADS, ROWS_AT_ONCE, LANES), F32)]
        + [two, two] + [one] * 8,
        scratch_shapes=[
            pltpu.VMEM((TABLE, 128), F32),
            pltpu.VMEM((ROWS_AT_ONCE * SLOTS, 128), F32),
            pltpu.VMEM((ROWS_AT_ONCE * PITCH, 128), F32),
            pltpu.VMEM((ROWS_AT_ONCE * PITCH, 128), F32),
            pltpu.VMEM((2 * ZW, LANES), F32),
            pltpu.VMEM((LANES, 2 * ZW), F32),
            pltpu.VMEM((2, batch, 2, PIECE, C), BF),
            pltpu.VMEM((2, batch, PIECE, C), BF),
            pltpu.VMEM((2, batch, PIECE, C), BF),
            pltpu.SemaphoreType.DMA((6,)),
            pltpu.SemaphoreType.DMA((6,)),
            pltpu.SemaphoreType.DMA((4,)),
        ],
        cost_estimate=pl.CostEstimate(flops=20_000_000, bytes_accessed=100_000_000, transcendentals=0),
        compiler_params=pltpu.CompilerParams(
            collective_id=0, has_side_effects=True, vmem_limit_bytes=60 << 20
        ),
        name="gather",
    )(position_index, tok, table, region_ids.reshape(2 * ZW, SLOTS), jnp.asarray(slots, BF))


def attend_kernel(
    lower_a, lower_b, upper_a, upper_b, right_a, right_b, left_a, left_b, order_ref, back_ref, w_qkv_ref, w_proj_ref, *rest
):
    bias_refs, rest = rest[:2], rest[2:]
    if len(rest) > 5:
        mid_left, mid_right, out_a, out_b, next_mid, prev_mid, own_scr, halo_scr, ctx_scr, send_sems, recv_sems = rest

        def blocks():
            return (
                remote(mid_left, next_mid, send_sems.at[0], recv_sems.at[0], "lon", -1),
                remote(mid_right, prev_mid, send_sems.at[1], recv_sems.at[1], "lon", 1),
            )

        @pl.when(pl.program_id(0) == 0)
        def _():
            greet(("lon",))
            greeted(("lon",))
            for block in blocks():
                block.start()
    else:
        blocks = None
        out_a, out_b, own_scr, halo_scr, ctx_scr = rest
    order = order_ref[...]

    def windows(top, bottom):
        return dot(order, jnp.concatenate([top, bottom], axis=0)).astype(BF)

    own = jnp.concatenate([windows(upper_a[0], upper_b[0]), windows(lower_a[0], lower_b[0])], axis=0)
    own_scr[...] = dot(own, w_qkv_ref[...])
    halo = jnp.concatenate([windows(right_a[0], right_b[0]), windows(left_a[0], left_b[0])], axis=0)
    halo_scr[...] = dot(halo, w_qkv_ref[:, C:])
    lane_head = lax.broadcasted_iota(jnp.int32, (1, 128), 1) // HEAD_DIM
    masks = [lane_head == h for h in range(4)]
    ones = jnp.ones((SLOTS, 128), BF)

    for zw in range(ZW):
        for side in range(2):
            rows = slice(side * CELLS + zw * HALF, side * CELLS + (zw + 1) * HALF)
            for g in range(3):
                lanes = slice(128 * g, 128 * g + 128)
                klanes = slice(C + 128 * g, C + 128 * g + 128)
                vlanes = slice(2 * C + 128 * g, 2 * C + 128 * g + 128)
                q = own_scr[rows, lanes] * (HEAD_DIM ** (-0.5) * LOG2E)
                stacked = jnp.concatenate([jnp.where(m, q, 0.0) for m in masks], axis=0).astype(BF)
                k = [own_scr[rows, klanes], halo_scr[rows, lanes]]
                v = [own_scr[rows, vlanes], halo_scr[rows, klanes]]
                if side == 1:
                    k, v = k[::-1], v[::-1]
                keys = jnp.concatenate(k, axis=0).astype(BF)
                values = jnp.concatenate([jnp.concatenate(v, axis=0).astype(BF), ones], axis=1)
                scores = lax.dot_general(stacked, keys, (((1,), (1,)), ((), ())), preferred_element_type=F32)
                bias = jnp.swapaxes(bias_refs[side][:, zw * HEADS + 4 * g : zw * HEADS + 4 * g + 4, :, :SLOTS], 0, 1)
                scores = scores + bias.reshape(4 * HALF, SLOTS)
                raised = jnp.exp2(scores - jnp.max(scores, axis=-1, keepdims=True)).astype(BF)
                both = dot(raised, values)
                top, total = both[:HALF, :128], both[:HALF, 128:]
                for h in range(1, 4):
                    top = jnp.where(masks[h], both[h * HALF : (h + 1) * HALF, :128], top)
                    total = jnp.where(masks[h], both[h * HALF : (h + 1) * HALF, 128:], total)
                ctx_scr[rows, lanes] = top / total
    back = back_ref[...]
    for side in range(2):
        natural = dot(back, ctx_scr[CELLS * side : CELLS * (side + 1), :].astype(BF)).astype(BF)
        result = dot(natural, w_proj_ref[...]).astype(BF)
        out_a[1 - side, 0] = result[:PIECE]
        out_b[1 - side, 0] = result[PIECE:]
    if blocks is not None:

        @pl.when(pl.program_id(0) == pl.num_programs(0) - 1)
        def _():
            for block in blocks():
                block.wait()


def attend(streams, order, w_qkv, w_proj, bias, lw, travelling=()):
    batch = streams[-1][0].shape[0]
    arrays, specs = [], []
    for array, dim, index in streams:
        arrays.append(array)
        if dim is None:
            specs.append(pl.BlockSpec((1, PIECE, C), lambda b: (b, 0, 0)))
        elif dim == 0:
            specs.append(pl.BlockSpec((None, 1, PIECE, C), lambda b, i=index: (i, b, 0, 0)))
        else:
            specs.append(pl.BlockSpec((1, None, PIECE, C), lambda b, i=index: (b, i, 0, 0)))
    anywhere = [pl.BlockSpec(memory_space=pl.ANY)] * len(travelling)
    sems = [pltpu.SemaphoreType.DMA((2,))] * len(travelling)
    remote_params = dict(collective_id=1, has_side_effects=True) if travelling else {}
    out = jax.ShapeDtypeStruct((2, batch, PIECE, C), BF)
    out_spec = pl.BlockSpec((2, 1, PIECE, C), lambda b: (0, b, 0, 0))
    return pl.pallas_call(
        attend_kernel,
        grid=(batch,),
        in_specs=specs
        + [
            full((CELLS, CELLS)),
            full((CELLS, CELLS)),
            full((C, 3 * C)),
            full((C, C)),
            pl.BlockSpec((STEPS // 2, ZW * HEADS, ROWS_AT_ONCE, LANES), lambda b: (0, lw, 0, 0)),
            pl.BlockSpec((STEPS // 2, ZW * HEADS, ROWS_AT_ONCE, LANES), lambda b: (1, lw, 0, 0)),
        ]
        + anywhere,
        out_specs=[out_spec, out_spec] + anywhere,
        out_shape=[out, out] + [jax.ShapeDtypeStruct(array.shape, BF) for array in travelling],
        scratch_shapes=[
            pltpu.VMEM((2 * CELLS, 3 * C), F32),
            pltpu.VMEM((2 * CELLS, 2 * C), F32),
            pltpu.VMEM((2 * CELLS, C), F32),
        ]
        + sems,
        cost_estimate=pl.CostEstimate(flops=20_000_000_000, bytes_accessed=16_000_000, transcendentals=4_000_000),
        compiler_params=pltpu.CompilerParams(vmem_limit_bytes=60 << 20, **remote_params),
        name="attend",
    )(*arrays, jnp.asarray(order, BF), jnp.asarray(order.T, BF), w_qkv, w_proj, bias, bias, *travelling)


CHUNK = 768


def feed_kernel(tok_ref, first_ref, mid_a, mid_b, last_ref, w_up_ref, w_down_ref, w_merge_ref, out_ref, hidden_scr):
    for piece, ref in enumerate((first_ref, mid_a, mid_b, last_ref)):
        for side in range(2):
            rows, cols = slice(3 * piece, 3 * piece + 3), slice(6 * side, 6 * side + 6)
            tok = tok_ref[0, rows, cols].astype(F32)
            attended = ref[side, 0].astype(F32).reshape(3, 6, ZL, C)
            hidden_scr[rows, cols] = (tok + attended).astype(BF).astype(F32)

    hidden = hidden_scr[...].reshape(12 * 12 * ZL, C)
    normed = normalized(hidden).astype(BF)
    block = hidden
    for f in range(0, FFN, CHUNK):
        up = dot(normed, w_up_ref[:, f : f + CHUNK])
        inner = (0.5 * up * (1.0 + lax.erf(up * 0.7071067811865476))).astype(BF)
        block = block + dot(inner, w_down_ref[f : f + CHUNK])
    block = block.astype(BF).astype(F32).reshape(6, 2, 6, 2, ZL, C)
    grouped = jnp.concatenate([block[:, p // 2, :, p % 2] for p in range(4)], axis=-1)
    grouped = normalized(grouped.reshape(36 * ZL, 4 * C)).astype(BF)
    out_ref[0] = dot(grouped, w_merge_ref[...]).reshape(6, 6, ZL, 2 * C).astype(BF)


def feed(tok, first, mid_a, mid_b, last, w_up, w_down, w_merge):
    batch = tok.shape[0]
    piece = pl.BlockSpec((2, 1, PIECE, C), lambda b: (0, b, 0, 0))
    return pl.pallas_call(
        feed_kernel,
        grid=(batch,),
        in_specs=[
            pl.BlockSpec((1, 12, 12, ZL, C), lambda b: (b, 0, 0, 0, 0)),
            piece,
            piece,
            piece,
            piece,
            full((C, FFN)),
            full((FFN, C)),
            full((4 * C, 2 * C)),
        ],
        out_specs=pl.BlockSpec((1, 6, 6, ZL, 2 * C), lambda b: (b, 0, 0, 0, 0)),
        out_shape=jax.ShapeDtypeStruct((batch, 6, 6, ZL, 2 * C), BF),
        scratch_shapes=[pltpu.VMEM((12, 12, ZL, C), F32)],
        cost_estimate=pl.CostEstimate(flops=14_000_000_000, bytes_accessed=14_000_000, transcendentals=7_000_000),
        compiler_params=pltpu.CompilerParams(vmem_limit_bytes=60 << 20),
        name="feed",
    )(tok, first, mid_a, mid_b, last, w_up, w_down, w_merge)


def on_device(tokens, w_qkv, w_proj, w_up, w_down, w_merge, earth_bias, position_index, region_ids):
    tok = jnp.transpose(tokens, (0, 2, 3, 1, 4))
    order = window_order()
    (
        bias, mid_left, mid_right, last_left, last_right, below_left, below_right,
        next_last, prev_last, next_below, prev_below,
    ) = gather(tok, earth_bias, position_index, region_ids)
    last_out, below_out, next_mid, prev_mid = attend(
        [
            (array, None, 0)
            for array in (
                last_left, below_left, last_right, below_right, next_last, next_below, prev_last, prev_below
            )
        ],
        order, w_qkv, w_proj, bias, 1, (mid_left, mid_right),
    )
    mid_a, mid_b = attend(
        [(array, 1, piece) for array in (mid_left, mid_right, next_mid, prev_mid) for piece in range(2)],
        order, w_qkv, w_proj, bias, 0,
    )
    first_out = passed_along(below_out, "lat", 1)
    merged = feed(tok, first_out, mid_a, mid_b, last_out, w_up, w_down, w_merge)
    return jnp.transpose(merged, (0, 3, 1, 2, 4))


def solution(mesh):
    in_specs = (
        P(None, None, "lat", "lon", None),
        P(),
        P(),
        P(),
        P(),
        P(),
        P("lat", None, None, None),
        P(),
        P("lat", None, None),
    )
    out_specs = P(None, None, "lat", "lon", None)
    return jax.shard_map(
        on_device, mesh=mesh, in_specs=in_specs, out_specs=out_specs, check_vma=False
    )
```

```python
import jax
import jax.numpy as jnp
import numpy as np
from jax import lax
from jax.experimental import pallas as pl
from jax.experimental.pallas import tpu as pltpu
from jax.sharding import PartitionSpec as P

HEADS = 12
HEAD_DIM = 32
C = 384
FFN = 1536
ZL = 8
ZW = 4
HALF = 72
SLOTS = 144
LANES = 256
CELLS = 288
PIECE = 144
LOG2E = 1.4426950408889634
BF = jnp.bfloat16
F32 = jnp.float32


def passed_along(block, axis, distance):
    devices = range(lax.axis_size(axis))
    route = [((i - distance) % len(devices), i) for i in devices]
    return lax.ppermute(block, axis, route)


def normalized(x):
    width = x.shape[-1]
    center = x - jnp.sum(x, axis=-1, keepdims=True) * (1.0 / width)
    spread = jnp.sum(center * center, axis=-1, keepdims=True) * (1.0 / width)
    return center * lax.rsqrt(spread + 1e-05)


def dot(a, b):
    return jnp.dot(a, b, preferred_element_type=F32)


def neighbour(axis, distance):
    size = lax.axis_size(axis)
    return {axis: lax.rem(lax.axis_index(axis) + distance + size, size)}


def remote(source, target, send_sem, recv_sem, axis, distance):
    return pltpu.make_async_remote_copy(
        src_ref=source,
        dst_ref=target,
        send_sem=send_sem,
        recv_sem=recv_sem,
        device_id=neighbour(axis, distance),
        device_id_type=pl.DeviceIdType.MESH,
    )


def greet(axes):
    barrier = pltpu.get_barrier_semaphore()
    for axis in axes:
        for distance in (-1, 1):
            pl.semaphore_signal(
                barrier, inc=1, device_id=neighbour(axis, distance), device_id_type=pl.DeviceIdType.MESH
            )


def greeted(axes):
    pl.semaphore_wait(pltpu.get_barrier_semaphore(), 2 * len(axes))


def full(shape):
    return pl.BlockSpec(shape, lambda *i: (0,) * len(shape))


ROWS_AT_ONCE = 8
STEPS = SLOTS // ROWS_AT_ONCE
TYPE_HEADS = 96
PITCH = 97
TABLE = 3312
ALONG = 4
FORWARD = 10
PICKS = 4


def slot_order():
    return np.arange(SLOTS, dtype=np.int32).reshape(2, 6, 2, 6).transpose(2, 1, 3, 0).reshape(-1)


def gather_kernel(
    index_ref, tok_ref, table_ref, labels_ref, slots_ref,
    out_ref, mid_left, mid_right, last_left, last_right, below_left, below_right,
    next_last, prev_last, next_below, prev_below,
    rows, picked, left, right, region_ref, region_col_ref, mids, firsts, lasts, send_sems, recv_sems, local_sems,
):
    step = pl.program_id(0)

    routes = (
        (firsts.at[0], below_left, "lat", -1),
        (firsts.at[1], below_right, "lat", -1),
        (lasts.at[0], next_last, "lon", -1),
        (lasts.at[1], prev_last, "lon", 1),
        (below_left, next_below, "lon", -1),
        (below_right, prev_below, "lon", 1),
    )

    def block(n):
        source, target, axis, distance = routes[n]
        return remote(source, target, send_sems.at[n], recv_sems.at[n], axis, distance)

    def local():
        pairs = (
            (mids.at[0], mid_left), (mids.at[1], mid_right), (lasts.at[0], last_left), (lasts.at[1], last_right)
        )
        return [pltpu.make_async_copy(a, b, local_sems.at[n]) for n, (a, b) in enumerate(pairs)]

    @pl.when(step == 0)
    def _():
        greet(("lat", "lon"))
        for piece, blocks in ((0, (firsts,)), (3, (lasts,)), (1, (mids, 0)), (2, (mids, 1))):
            for b in range(tok_ref.shape[0]):
                x = normalized(tok_ref[b, 3 * piece : 3 * piece + 3].astype(F32))
                for side in range(2):
                    part = x[:, 6 * side : 6 * side + 6].reshape(PIECE, C).astype(BF)
                    if len(blocks) == 1:
                        blocks[0][side, b] = part
                    else:
                        blocks[0][side, b, blocks[1]] = part
            if piece == 0:
                greeted(("lat", "lon"))
                block(0).start()
                block(1).start()
        for copy in local():
            copy.start()
        for c in range(0, TABLE, 128):
            width = min(128, TABLE - c)
            some = table_ref[:, :, :, c : c + width].reshape(TYPE_HEADS, width)
            rows[c : c + width, :TYPE_HEADS] = some.T
        labels = dot((labels_ref[...] + 1).astype(F32).astype(BF), slots_ref[...])
        region_ref[...] = labels
        region_col_ref[...] = labels.T

    @pl.when(step == ALONG)
    def _():
        block(2).start()
        block(3).start()

    @pl.when(step == FORWARD)
    def _():
        for n in range(2):
            block(n).wait_recv()
            block(4 + n).start()

    order = [int(n) for n in slot_order()]

    def pick(turn, carry):
        for j in range(PICKS):
            row = step * ROWS_AT_ONCE + turn * (PICKS // 2) + j // 2
            side, place = row // HALF, row % HALF
            slot = place % 2 * 72 + place // 12 * 12 + side * 6 + place // 2 % 6
            base = pl.multiple_of(turn * (PICKS * HALF) + j * HALF, 8)
            for k in range(HALF):
                picked[pl.ds(base + k, 1), :] = rows[pl.ds(index_ref[slot, order[j % 2 * HALF + k]], 1), :]
        return carry

    lax.fori_loop(0, ROWS_AT_ONCE * 2 // PICKS, pick, 0)
    for s in range(ROWS_AT_ONCE):
        left[PITCH * s : PITCH * s + TYPE_HEADS, :] = picked[SLOTS * s : SLOTS * s + 128, :].T[:TYPE_HEADS]
        right[PITCH * s : PITCH * s + TYPE_HEADS, :16] = picked[SLOTS * s + 128 : SLOTS * (s + 1), :].T[:TYPE_HEADS]
    for lw in range(2):
        for zw in range(ZW):
            kind = lw * ZW + zw
            same = region_col_ref[pl.ds(pl.multiple_of(step * ROWS_AT_ONCE, 8), ROWS_AT_ONCE), kind : kind + 1] == region_ref[kind : kind + 1, :]
            for h in range(HEADS):
                source = (lw * HEADS + h) * ZW + zw
                place = kind * HEADS + h
                out_ref[0, place, :, :128] = jnp.where(
                    same[:, :128], left[pl.ds(source, ROWS_AT_ONCE, stride=PITCH), :] * LOG2E, -1e9
                )
                out_ref[0, place, :, 128:] = jnp.where(
                    same[:, 128:], right[pl.ds(source, ROWS_AT_ONCE, stride=PITCH), :] * LOG2E, -1e9
                )

    @pl.when(step == STEPS - 1)
    def _():
        for n in range(6):
            block(n).wait_send()
            if n >= 2:
                block(n).wait_recv()
        for copy in local():
            copy.wait()


def gather(tok, earth_bias, position_index, region_ids):
    batch = tok.shape[0]
    table = jnp.transpose(earth_bias, (0, 3, 1, 2))
    slots = np.zeros((SLOTS, LANES), np.float32)
    slots[slot_order(), np.arange(SLOTS)] = 1.0
    two, one = jax.ShapeDtypeStruct((batch, 2, PIECE, C), BF), jax.ShapeDtypeStruct((batch, PIECE, C), BF)
    anywhere = pl.BlockSpec(memory_space=pl.ANY)
    return pl.pallas_call(
        gather_kernel,
        grid=(STEPS,),
        in_specs=[
            pl.BlockSpec(memory_space=pltpu.SMEM),
            full(tok.shape),
            full(table.shape),
            full((2 * ZW, SLOTS)),
            full((SLOTS, LANES)),
        ],
        out_specs=[pl.BlockSpec((1, TYPE_HEADS, ROWS_AT_ONCE, LANES), lambda i: (i, 0, 0, 0))] + [anywhere] * 10,
        out_shape=[jax.ShapeDtypeStruct((STEPS, TYPE_HEADS, ROWS_AT_ONCE, LANES), F32)]
        + [two, two] + [one] * 8,
        scratch_shapes=[
            pltpu.VMEM((TABLE, 128), F32),
            pltpu.VMEM((ROWS_AT_ONCE * SLOTS, 128), F32),
            pltpu.VMEM((ROWS_AT_ONCE * PITCH, 128), F32),
            pltpu.VMEM((ROWS_AT_ONCE * PITCH, 128), F32),
            pltpu.VMEM((2 * ZW, LANES), F32),
            pltpu.VMEM((LANES, 2 * ZW), F32),
            pltpu.VMEM((2, batch, 2, PIECE, C), BF),
            pltpu.VMEM((2, batch, PIECE, C), BF),
            pltpu.VMEM((2, batch, PIECE, C), BF),
            pltpu.SemaphoreType.DMA((6,)),
            pltpu.SemaphoreType.DMA((6,)),
            pltpu.SemaphoreType.DMA((4,)),
        ],
        cost_estimate=pl.CostEstimate(flops=20_000_000, bytes_accessed=100_000_000, transcendentals=0),
        compiler_params=pltpu.CompilerParams(
            collective_id=0, has_side_effects=True, vmem_limit_bytes=60 << 20
        ),
        name="gather",
    )(position_index, tok, table, region_ids.reshape(2 * ZW, SLOTS), jnp.asarray(slots, BF))


def attend_kernel(
    lower_a, lower_b, upper_a, upper_b, right_a, right_b, left_a, left_b, w_qkv_ref, w_proj_ref, *rest
):
    bias_refs, rest = rest[:2], rest[2:]
    if len(rest) > 5:
        mid_left, mid_right, out_a, out_b, next_mid, prev_mid, own_scr, halo_scr, ctx_scr, send_sems, recv_sems = rest

        def blocks():
            return (
                remote(mid_left, next_mid, send_sems.at[0], recv_sems.at[0], "lon", -1),
                remote(mid_right, prev_mid, send_sems.at[1], recv_sems.at[1], "lon", 1),
            )

        @pl.when(pl.program_id(0) == 0)
        def _():
            greet(("lon",))
            greeted(("lon",))
            for block in blocks():
                block.start()
    else:
        blocks = None
        out_a, out_b, own_scr, halo_scr, ctx_scr = rest
    level = lax.broadcasted_iota(jnp.int32, (1, ZL, 128), 1)
    level = jnp.concatenate([level] * 3, axis=-1)

    def chosen(parts, which):
        result = parts[0]
        for n in range(1, 4):
            result = jnp.where(which == n, parts[n], result)
        return result

    def windows(top, bottom):
        x = jnp.concatenate([top, bottom], axis=0).astype(F32).reshape(9, 4, ZL, C)
        result = []
        for zw in range(ZW):
            parts = [pltpu.roll(x[:, i], (2 * i - 2 * zw - 1) % ZL, axis=1) for i in range(4)]
            result.append(chosen(parts, level // 2).reshape(HALF, C))
        return jnp.concatenate(result, axis=0).astype(BF)

    def natural(x):
        result = []
        for i in range(4):
            parts = [
                pltpu.roll(x[zw * HALF : (zw + 1) * HALF].reshape(9, ZL, C), (2 * zw + 1 - 2 * i) % ZL, axis=1)
                for zw in range(ZW)
            ]
            result.append(chosen(parts, (level + ZL - 1) % ZL // 2))
        return jnp.stack(result, axis=1).reshape(CELLS, C)

    own = jnp.concatenate([windows(upper_a[0], upper_b[0]), windows(lower_a[0], lower_b[0])], axis=0)
    own_scr[...] = dot(own, w_qkv_ref[...])
    halo = jnp.concatenate([windows(right_a[0], right_b[0]), windows(left_a[0], left_b[0])], axis=0)
    halo_scr[...] = dot(halo, w_qkv_ref[:, C:])
    lane_head = lax.broadcasted_iota(jnp.int32, (1, 128), 1) // HEAD_DIM
    masks = [lane_head == h for h in range(4)]
    ones = jnp.ones((SLOTS, 128), BF)

    for zw in range(ZW):
        for side in range(2):
            rows = slice(side * CELLS + zw * HALF, side * CELLS + (zw + 1) * HALF)
            for g in range(3):
                lanes = slice(128 * g, 128 * g + 128)
                klanes = slice(C + 128 * g, C + 128 * g + 128)
                vlanes = slice(2 * C + 128 * g, 2 * C + 128 * g + 128)
                q = own_scr[rows, lanes] * (HEAD_DIM ** (-0.5) * LOG2E)
                stacked = jnp.concatenate([jnp.where(m, q, 0.0) for m in masks], axis=0).astype(BF)
                k = [own_scr[rows, klanes], halo_scr[rows, lanes]]
                v = [own_scr[rows, vlanes], halo_scr[rows, klanes]]
                if side == 1:
                    k, v = k[::-1], v[::-1]
                keys = jnp.concatenate(k, axis=0).astype(BF)
                values = jnp.concatenate([jnp.concatenate(v, axis=0).astype(BF), ones], axis=1)
                scores = lax.dot_general(stacked, keys, (((1,), (1,)), ((), ())), preferred_element_type=F32)
                bias = jnp.swapaxes(bias_refs[side][:, zw * HEADS + 4 * g : zw * HEADS + 4 * g + 4, :, :SLOTS], 0, 1)
                scores = scores + bias.reshape(4 * HALF, SLOTS)
                raised = jnp.exp2(scores - jnp.max(scores, axis=-1, keepdims=True)).astype(BF)
                both = dot(raised, values)
                top, total = both[:HALF, :128], both[:HALF, 128:]
                for h in range(1, 4):
                    top = jnp.where(masks[h], both[h * HALF : (h + 1) * HALF, :128], top)
                    total = jnp.where(masks[h], both[h * HALF : (h + 1) * HALF, 128:], total)
                ctx_scr[rows, lanes] = top / total
    for side in range(2):
        context = natural(ctx_scr[CELLS * side : CELLS * (side + 1), :]).astype(BF)
        result = dot(context, w_proj_ref[...]).astype(BF)
        out_a[1 - side, 0] = result[:PIECE]
        out_b[1 - side, 0] = result[PIECE:]
    if blocks is not None:

        @pl.when(pl.program_id(0) == pl.num_programs(0) - 1)
        def _():
            for block in blocks():
                block.wait()


def attend(streams, w_qkv, w_proj, bias, lw, travelling=()):
    batch = streams[-1][0].shape[0]
    arrays, specs = [], []
    for array, dim, index in streams:
        arrays.append(array)
        if dim is None:
            specs.append(pl.BlockSpec((1, PIECE, C), lambda b: (b, 0, 0)))
        elif dim == 0:
            specs.append(pl.BlockSpec((None, 1, PIECE, C), lambda b, i=index: (i, b, 0, 0)))
        else:
            specs.append(pl.BlockSpec((1, None, PIECE, C), lambda b, i=index: (b, i, 0, 0)))
    anywhere = [pl.BlockSpec(memory_space=pl.ANY)] * len(travelling)
    sems = [pltpu.SemaphoreType.DMA((2,))] * len(travelling)
    remote_params = dict(collective_id=1, has_side_effects=True) if travelling else {}
    out = jax.ShapeDtypeStruct((2, batch, PIECE, C), BF)
    out_spec = pl.BlockSpec((2, 1, PIECE, C), lambda b: (0, b, 0, 0))
    return pl.pallas_call(
        attend_kernel,
        grid=(batch,),
        in_specs=specs
        + [
            full((C, 3 * C)),
            full((C, C)),
            pl.BlockSpec((STEPS // 2, ZW * HEADS, ROWS_AT_ONCE, LANES), lambda b: (0, lw, 0, 0)),
            pl.BlockSpec((STEPS // 2, ZW * HEADS, ROWS_AT_ONCE, LANES), lambda b: (1, lw, 0, 0)),
        ]
        + anywhere,
        out_specs=[out_spec, out_spec] + anywhere,
        out_shape=[out, out] + [jax.ShapeDtypeStruct(array.shape, BF) for array in travelling],
        scratch_shapes=[
            pltpu.VMEM((2 * CELLS, 3 * C), F32),
            pltpu.VMEM((2 * CELLS, 2 * C), F32),
            pltpu.VMEM((2 * CELLS, C), F32),
        ]
        + sems,
        cost_estimate=pl.CostEstimate(flops=20_000_000_000, bytes_accessed=16_000_000, transcendentals=4_000_000),
        compiler_params=pltpu.CompilerParams(vmem_limit_bytes=60 << 20, **remote_params),
        name="attend",
    )(*arrays, w_qkv, w_proj, bias, bias, *travelling)


CHUNK = 768


def feed_kernel(tok_ref, first_ref, mid_a, mid_b, last_ref, w_up_ref, w_down_ref, w_merge_ref, out_ref, hidden_scr):
    for piece, ref in enumerate((first_ref, mid_a, mid_b, last_ref)):
        for side in range(2):
            rows, cols = slice(3 * piece, 3 * piece + 3), slice(6 * side, 6 * side + 6)
            tok = tok_ref[0, rows, cols].astype(F32)
            attended = ref[side, 0].astype(F32).reshape(3, 6, ZL, C)
            hidden_scr[rows, cols] = (tok + attended).astype(BF).astype(F32)

    hidden = hidden_scr[...].reshape(12 * 12 * ZL, C)
    normed = normalized(hidden).astype(BF)
    block = hidden
    for f in range(0, FFN, CHUNK):
        up = dot(normed, w_up_ref[:, f : f + CHUNK])
        inner = (0.5 * up * (1.0 + lax.erf(up * 0.7071067811865476))).astype(BF)
        block = block + dot(inner, w_down_ref[f : f + CHUNK])
    block = block.astype(BF).astype(F32).reshape(6, 2, 6, 2, ZL, C)
    grouped = jnp.concatenate([block[:, p // 2, :, p % 2] for p in range(4)], axis=-1)
    grouped = normalized(grouped.reshape(36 * ZL, 4 * C)).astype(BF)
    out_ref[0] = dot(grouped, w_merge_ref[...]).reshape(6, 6, ZL, 2 * C).astype(BF)


def feed(tok, first, mid_a, mid_b, last, w_up, w_down, w_merge):
    batch = tok.shape[0]
    piece = pl.BlockSpec((2, 1, PIECE, C), lambda b: (0, b, 0, 0))
    return pl.pallas_call(
        feed_kernel,
        grid=(batch,),
        in_specs=[
            pl.BlockSpec((1, 12, 12, ZL, C), lambda b: (b, 0, 0, 0, 0)),
            piece,
            piece,
            piece,
            piece,
            full((C, FFN)),
            full((FFN, C)),
            full((4 * C, 2 * C)),
        ],
        out_specs=pl.BlockSpec((1, 6, 6, ZL, 2 * C), lambda b: (b, 0, 0, 0, 0)),
        out_shape=jax.ShapeDtypeStruct((batch, 6, 6, ZL, 2 * C), BF),
        scratch_shapes=[pltpu.VMEM((12, 12, ZL, C), F32)],
        cost_estimate=pl.CostEstimate(flops=14_000_000_000, bytes_accessed=14_000_000, transcendentals=7_000_000),
        compiler_params=pltpu.CompilerParams(vmem_limit_bytes=60 << 20),
        name="feed",
    )(tok, first, mid_a, mid_b, last, w_up, w_down, w_merge)


def on_device(tokens, w_qkv, w_proj, w_up, w_down, w_merge, earth_bias, position_index, region_ids):
    tok = jnp.transpose(tokens, (0, 2, 3, 1, 4))
    (
        bias, mid_left, mid_right, last_left, last_right, below_left, below_right,
        next_last, prev_last, next_below, prev_below,
    ) = gather(tok, earth_bias, position_index, region_ids)
    last_out, below_out, next_mid, prev_mid = attend(
        [
            (array, None, 0)
            for array in (
                last_left, below_left, last_right, below_right, next_last, next_below, prev_last, prev_below
            )
        ],
        w_qkv, w_proj, bias, 1, (mid_left, mid_right),
    )
    mid_a, mid_b = attend(
        [(array, 1, piece) for array in (mid_left, mid_right, next_mid, prev_mid) for piece in range(2)],
        w_qkv, w_proj, bias, 0,
    )
    first_out = passed_along(below_out, "lat", 1)
    merged = feed(tok, first_out, mid_a, mid_b, last_out, w_up, w_down, w_merge)
    return jnp.transpose(merged, (0, 3, 1, 2, 4))


def solution(mesh):
    in_specs = (
        P(None, None, "lat", "lon", None),
        P(),
        P(),
        P(),
        P(),
        P(),
        P("lat", None, None, None),
        P(),
        P("lat", None, None),
    )
    out_specs = P(None, None, "lat", "lon", None)
    return jax.shard_map(
        on_device, mesh=mesh, in_specs=in_specs, out_specs=out_specs, check_vma=False
    )
```

```python
import jax
import jax.numpy as jnp
import numpy as np
from jax import lax
from jax.experimental import pallas as pl
from jax.experimental.pallas import tpu as pltpu
from jax.sharding import PartitionSpec as P

HEADS = 12
HEAD_DIM = 32
C = 384
FFN = 1536
ZL = 8
ZW = 4
HALF = 72
SLOTS = 144
LANES = 256
CELLS = 288
PIECE = 144
LOG2E = 1.4426950408889634
BF = jnp.bfloat16
F32 = jnp.float32


def passed_along(block, axis, distance):
    devices = range(lax.axis_size(axis))
    route = [((i - distance) % len(devices), i) for i in devices]
    return lax.ppermute(block, axis, route)


def normalized(x):
    width = x.shape[-1]
    center = x - jnp.sum(x, axis=-1, keepdims=True) * (1.0 / width)
    spread = jnp.sum(center * center, axis=-1, keepdims=True) * (1.0 / width)
    return center * lax.rsqrt(spread + 1e-05)


def dot(a, b):
    return jnp.dot(a, b, preferred_element_type=F32)


def neighbour(axis, distance):
    size = lax.axis_size(axis)
    return {axis: lax.rem(lax.axis_index(axis) + distance + size, size)}


def remote(source, target, send_sem, recv_sem, axis, distance):
    return pltpu.make_async_remote_copy(
        src_ref=source,
        dst_ref=target,
        send_sem=send_sem,
        recv_sem=recv_sem,
        device_id=neighbour(axis, distance),
        device_id_type=pl.DeviceIdType.MESH,
    )


def greet(axes):
    barrier = pltpu.get_barrier_semaphore()
    for axis in axes:
        for distance in (-1, 1):
            pl.semaphore_signal(
                barrier, inc=1, device_id=neighbour(axis, distance), device_id_type=pl.DeviceIdType.MESH
            )


def greeted(axes):
    pl.semaphore_wait(pltpu.get_barrier_semaphore(), 2 * len(axes))


def full(shape):
    return pl.BlockSpec(shape, lambda *i: (0,) * len(shape))


ROWS_AT_ONCE = 8
STEPS = SLOTS // ROWS_AT_ONCE
TYPE_HEADS = 96
PITCH = 97
TABLE = 3312
ALONG = 4
FORWARD = 10
PICKS = 4


def slot_order():
    return np.arange(SLOTS, dtype=np.int32).reshape(2, 6, 2, 6).transpose(2, 1, 3, 0).reshape(-1)


def gather_kernel(
    index_ref, tok_ref, table_ref, labels_ref, slots_ref,
    out_ref, mid_left_a, mid_left_b, mid_right_a, mid_right_b, last_left, last_right, below_left, below_right,
    next_mid_a, prev_mid_a, next_last, prev_last, next_below, prev_below,
    rows, picked, left, right, region_ref, region_col_ref, mids, firsts, lasts, send_sems, recv_sems, local_sems,
):
    step = pl.program_id(0)

    routes = (
        (firsts.at[0], below_left, "lat", -1),
        (firsts.at[1], below_right, "lat", -1),
        (lasts.at[0], next_last, "lon", -1),
        (lasts.at[1], prev_last, "lon", 1),
        (below_left, next_below, "lon", -1),
        (below_right, prev_below, "lon", 1),
        (mids.at[0, 0], next_mid_a, "lon", -1),
        (mids.at[0, 1], prev_mid_a, "lon", 1),
    )

    def block(n):
        source, target, axis, distance = routes[n]
        return remote(source, target, send_sems.at[n], recv_sems.at[n], axis, distance)

    def local():
        pairs = (
            (mids.at[0, 0], mid_left_a), (mids.at[0, 1], mid_right_a),
            (mids.at[1, 0], mid_left_b), (mids.at[1, 1], mid_right_b),
            (lasts.at[0], last_left), (lasts.at[1], last_right),
        )
        return [pltpu.make_async_copy(a, b, local_sems.at[n]) for n, (a, b) in enumerate(pairs)]

    @pl.when(step == 0)
    def _():
        greet(("lat", "lon"))
        for piece, blocks in ((0, firsts), (3, lasts), (1, mids.at[0]), (2, mids.at[1])):
            for b in range(tok_ref.shape[0]):
                x = normalized(tok_ref[b, 3 * piece : 3 * piece + 3].astype(F32))
                for side in range(2):
                    part = x[:, 6 * side : 6 * side + 6].reshape(PIECE, C).astype(BF)
                    blocks[side, b] = part
            if piece == 0:
                greeted(("lat", "lon"))
                block(0).start()
                block(1).start()
        for copy in local():
            copy.start()
        for c in range(0, TABLE, 128):
            width = min(128, TABLE - c)
            some = table_ref[:, :, :, c : c + width].reshape(TYPE_HEADS, width)
            rows[c : c + width, :TYPE_HEADS] = some.T
        labels = dot((labels_ref[...] + 1).astype(F32).astype(BF), slots_ref[...])
        region_ref[...] = labels
        region_col_ref[...] = labels.T

    @pl.when(step == ALONG)
    def _():
        for n in (2, 3, 6, 7):
            block(n).start()

    @pl.when(step == FORWARD)
    def _():
        for n in range(2):
            block(n).wait_recv()
            block(4 + n).start()

    order = [int(n) for n in slot_order()]

    def pick(turn, carry):
        for j in range(PICKS):
            row = step * ROWS_AT_ONCE + turn * (PICKS // 2) + j // 2
            side, place = row // HALF, row % HALF
            slot = place % 2 * 72 + place // 12 * 12 + side * 6 + place // 2 % 6
            base = pl.multiple_of(turn * (PICKS * HALF) + j * HALF, 8)
            for k in range(HALF):
                picked[pl.ds(base + k, 1), :] = rows[pl.ds(index_ref[slot, order[j % 2 * HALF + k]], 1), :]
        return carry

    lax.fori_loop(0, ROWS_AT_ONCE * 2 // PICKS, pick, 0)
    for s in range(ROWS_AT_ONCE):
        left[PITCH * s : PITCH * s + TYPE_HEADS, :] = picked[SLOTS * s : SLOTS * s + 128, :].T[:TYPE_HEADS]
        right[PITCH * s : PITCH * s + TYPE_HEADS, :16] = picked[SLOTS * s + 128 : SLOTS * (s + 1), :].T[:TYPE_HEADS]
    for lw in range(2):
        for zw in range(ZW):
            kind = lw * ZW + zw
            same = region_col_ref[pl.ds(pl.multiple_of(step * ROWS_AT_ONCE, 8), ROWS_AT_ONCE), kind : kind + 1] == region_ref[kind : kind + 1, :]
            for h in range(HEADS):
                source = (lw * HEADS + h) * ZW + zw
                place = kind * HEADS + h
                out_ref[0, place, :, :128] = jnp.where(
                    same[:, :128], left[pl.ds(source, ROWS_AT_ONCE, stride=PITCH), :] * LOG2E, -1e9
                )
                out_ref[0, place, :, 128:] = jnp.where(
                    same[:, 128:], right[pl.ds(source, ROWS_AT_ONCE, stride=PITCH), :] * LOG2E, -1e9
                )

    @pl.when(step == STEPS - 1)
    def _():
        for n in range(8):
            block(n).wait_send()
            if n >= 2:
                block(n).wait_recv()
        for copy in local():
            copy.wait()


def gather(tok, earth_bias, position_index, region_ids):
    batch = tok.shape[0]
    table = jnp.transpose(earth_bias, (0, 3, 1, 2))
    slots = np.zeros((SLOTS, LANES), np.float32)
    slots[slot_order(), np.arange(SLOTS)] = 1.0
    one = jax.ShapeDtypeStruct((batch, PIECE, C), BF)
    anywhere = pl.BlockSpec(memory_space=pl.ANY)
    return pl.pallas_call(
        gather_kernel,
        grid=(STEPS,),
        in_specs=[
            pl.BlockSpec(memory_space=pltpu.SMEM),
            full(tok.shape),
            full(table.shape),
            full((2 * ZW, SLOTS)),
            full((SLOTS, LANES)),
        ],
        out_specs=[pl.BlockSpec((1, TYPE_HEADS, ROWS_AT_ONCE, LANES), lambda i: (i, 0, 0, 0))] + [anywhere] * 14,
        out_shape=[jax.ShapeDtypeStruct((STEPS, TYPE_HEADS, ROWS_AT_ONCE, LANES), F32)]
        + [one] * 14,
        scratch_shapes=[
            pltpu.VMEM((TABLE, 128), F32),
            pltpu.VMEM((ROWS_AT_ONCE * SLOTS, 128), F32),
            pltpu.VMEM((ROWS_AT_ONCE * PITCH, 128), F32),
            pltpu.VMEM((ROWS_AT_ONCE * PITCH, 128), F32),
            pltpu.VMEM((2 * ZW, LANES), F32),
            pltpu.VMEM((LANES, 2 * ZW), F32),
            pltpu.VMEM((2, 2, batch, PIECE, C), BF),
            pltpu.VMEM((2, batch, PIECE, C), BF),
            pltpu.VMEM((2, batch, PIECE, C), BF),
            pltpu.SemaphoreType.DMA((8,)),
            pltpu.SemaphoreType.DMA((8,)),
            pltpu.SemaphoreType.DMA((6,)),
        ],
        cost_estimate=pl.CostEstimate(flops=20_000_000, bytes_accessed=100_000_000, transcendentals=0),
        compiler_params=pltpu.CompilerParams(
            collective_id=0, has_side_effects=True, vmem_limit_bytes=60 << 20
        ),
        name="gather",
    )(position_index, tok, table, region_ids.reshape(2 * ZW, SLOTS), jnp.asarray(slots, BF))


def attend_kernel(
    lower_a, lower_b, upper_a, upper_b, right_a, right_b, left_a, left_b, w_qkv_ref, w_proj_ref, *rest
):
    bias_refs, rest = rest[:2], rest[2:]
    if len(rest) > 5:
        mid_left, mid_right, out_a, out_b, next_mid, prev_mid, own_scr, halo_scr, ctx_scr, send_sems, recv_sems = rest

        def blocks():
            return (
                remote(mid_left, next_mid, send_sems.at[0], recv_sems.at[0], "lon", -1),
                remote(mid_right, prev_mid, send_sems.at[1], recv_sems.at[1], "lon", 1),
            )

        @pl.when(pl.program_id(0) == 0)
        def _():
            greet(("lon",))

        @pl.when(pl.program_id(0) == 1)
        def _():
            greeted(("lon",))
            for block in blocks():
                block.start()
    else:
        blocks = None
        out_a, out_b, own_scr, halo_scr, ctx_scr = rest
    level = lax.broadcasted_iota(jnp.int32, (1, ZL, 128), 1)
    level = jnp.concatenate([level] * 3, axis=-1)

    def chosen(parts, which):
        result = parts[0]
        for n in range(1, 4):
            result = jnp.where(which == n, parts[n], result)
        return result

    def windows(top, bottom):
        x = jnp.concatenate([top, bottom], axis=0).astype(F32).reshape(9, 4, ZL, C)
        result = []
        for zw in range(ZW):
            parts = [pltpu.roll(x[:, i], (2 * i - 2 * zw - 1) % ZL, axis=1) for i in range(4)]
            result.append(chosen(parts, level // 2).reshape(HALF, C))
        return jnp.concatenate(result, axis=0).astype(BF)

    def natural(x):
        result = []
        for i in range(4):
            parts = [
                pltpu.roll(x[zw * HALF : (zw + 1) * HALF].reshape(9, ZL, C), (2 * zw + 1 - 2 * i) % ZL, axis=1)
                for zw in range(ZW)
            ]
            result.append(chosen(parts, (level + ZL - 1) % ZL // 2))
        return jnp.stack(result, axis=1).reshape(CELLS, C)

    own = jnp.concatenate([windows(upper_a[0], upper_b[0]), windows(lower_a[0], lower_b[0])], axis=0)
    own_scr[...] = dot(own, w_qkv_ref[...])
    halo = jnp.concatenate([windows(right_a[0], right_b[0]), windows(left_a[0], left_b[0])], axis=0)
    halo_scr[...] = dot(halo, w_qkv_ref[:, C:])
    lane_head = lax.broadcasted_iota(jnp.int32, (1, 128), 1) // HEAD_DIM
    masks = [lane_head == h for h in range(4)]
    ones = jnp.ones((SLOTS, 128), BF)

    for zw in range(ZW):
        for side in range(2):
            rows = slice(side * CELLS + zw * HALF, side * CELLS + (zw + 1) * HALF)
            for g in range(3):
                lanes = slice(128 * g, 128 * g + 128)
                klanes = slice(C + 128 * g, C + 128 * g + 128)
                vlanes = slice(2 * C + 128 * g, 2 * C + 128 * g + 128)
                q = own_scr[rows, lanes] * (HEAD_DIM ** (-0.5) * LOG2E)
                stacked = jnp.concatenate([jnp.where(m, q, 0.0) for m in masks], axis=0).astype(BF)
                k = [own_scr[rows, klanes], halo_scr[rows, lanes]]
                v = [own_scr[rows, vlanes], halo_scr[rows, klanes]]
                if side == 1:
                    k, v = k[::-1], v[::-1]
                keys = jnp.concatenate(k, axis=0).astype(BF)
                values = jnp.concatenate([jnp.concatenate(v, axis=0).astype(BF), ones], axis=1)
                scores = lax.dot_general(stacked, keys, (((1,), (1,)), ((), ())), preferred_element_type=F32)
                bias = jnp.swapaxes(bias_refs[side][:, zw * HEADS + 4 * g : zw * HEADS + 4 * g + 4, :, :SLOTS], 0, 1)
                scores = scores + bias.reshape(4 * HALF, SLOTS)
                raised = jnp.exp2(scores - jnp.max(scores, axis=-1, keepdims=True)).astype(BF)
                both = dot(raised, values)
                top, total = both[:HALF, :128], both[:HALF, 128:]
                for h in range(1, 4):
                    top = jnp.where(masks[h], both[h * HALF : (h + 1) * HALF, :128], top)
                    total = jnp.where(masks[h], both[h * HALF : (h + 1) * HALF, 128:], total)
                ctx_scr[rows, lanes] = top / total
    for side in range(2):
        context = natural(ctx_scr[CELLS * side : CELLS * (side + 1), :]).astype(BF)
        result = dot(context, w_proj_ref[...]).astype(BF)
        out_a[1 - side, 0] = result[:PIECE]
        out_b[1 - side, 0] = result[PIECE:]
    if blocks is not None:

        @pl.when(pl.program_id(0) == pl.num_programs(0) - 1)
        def _():
            for block in blocks():
                block.wait()


def attend(streams, w_qkv, w_proj, bias, lw, travelling=()):
    batch = streams[0].shape[0]
    specs = [pl.BlockSpec((1, PIECE, C), lambda b: (b, 0, 0))] * len(streams)
    anywhere = [pl.BlockSpec(memory_space=pl.ANY)] * len(travelling)
    sems = [pltpu.SemaphoreType.DMA((2,))] * len(travelling)
    remote_params = dict(collective_id=1, has_side_effects=True) if travelling else {}
    out = jax.ShapeDtypeStruct((2, batch, PIECE, C), BF)
    out_spec = pl.BlockSpec((2, 1, PIECE, C), lambda b: (0, b, 0, 0))
    return pl.pallas_call(
        attend_kernel,
        grid=(batch,),
        in_specs=specs
        + [
            full((C, 3 * C)),
            full((C, C)),
            pl.BlockSpec((STEPS // 2, ZW * HEADS, ROWS_AT_ONCE, LANES), lambda b: (0, lw, 0, 0)),
            pl.BlockSpec((STEPS // 2, ZW * HEADS, ROWS_AT_ONCE, LANES), lambda b: (1, lw, 0, 0)),
        ]
        + anywhere,
        out_specs=[out_spec, out_spec] + anywhere,
        out_shape=[out, out] + [jax.ShapeDtypeStruct(array.shape, BF) for array in travelling],
        scratch_shapes=[
            pltpu.VMEM((2 * CELLS, 3 * C), F32),
            pltpu.VMEM((2 * CELLS, 2 * C), F32),
            pltpu.VMEM((2 * CELLS, C), F32),
        ]
        + sems,
        cost_estimate=pl.CostEstimate(flops=20_000_000_000, bytes_accessed=16_000_000, transcendentals=4_000_000),
        compiler_params=pltpu.CompilerParams(vmem_limit_bytes=60 << 20, **remote_params),
        name="attend",
    )(*streams, w_qkv, w_proj, bias, bias, *travelling)


CHUNK = 768


def feed_kernel(tok_ref, first_ref, mid_a, mid_b, last_ref, w_up_ref, w_down_ref, w_merge_ref, out_ref, hidden_scr):
    for piece, ref in enumerate((first_ref, mid_a, mid_b, last_ref)):
        for side in range(2):
            rows, cols = slice(3 * piece, 3 * piece + 3), slice(6 * side, 6 * side + 6)
            tok = tok_ref[0, rows, cols].astype(F32)
            attended = ref[side, 0].astype(F32).reshape(3, 6, ZL, C)
            hidden_scr[rows, cols] = (tok + attended).astype(BF).astype(F32)

    hidden = hidden_scr[...].reshape(12 * 12 * ZL, C)
    normed = normalized(hidden).astype(BF)
    block = hidden
    for f in range(0, FFN, CHUNK):
        up = dot(normed, w_up_ref[:, f : f + CHUNK])
        inner = (0.5 * up * (1.0 + lax.erf(up * 0.7071067811865476))).astype(BF)
        block = block + dot(inner, w_down_ref[f : f + CHUNK])
    block = block.astype(BF).astype(F32).reshape(6, 2, 6, 2, ZL, C)
    grouped = jnp.concatenate([block[:, p // 2, :, p % 2] for p in range(4)], axis=-1)
    grouped = normalized(grouped.reshape(36 * ZL, 4 * C)).astype(BF)
    out_ref[0] = dot(grouped, w_merge_ref[...]).reshape(6, 6, ZL, 2 * C).astype(BF)


def feed(tok, first, mid_a, mid_b, last, w_up, w_down, w_merge):
    batch = tok.shape[0]
    piece = pl.BlockSpec((2, 1, PIECE, C), lambda b: (0, b, 0, 0))
    return pl.pallas_call(
        feed_kernel,
        grid=(batch,),
        in_specs=[
            pl.BlockSpec((1, 12, 12, ZL, C), lambda b: (b, 0, 0, 0, 0)),
            piece,
            piece,
            piece,
            piece,
            full((C, FFN)),
            full((FFN, C)),
            full((4 * C, 2 * C)),
        ],
        out_specs=pl.BlockSpec((1, 6, 6, ZL, 2 * C), lambda b: (b, 0, 0, 0, 0)),
        out_shape=jax.ShapeDtypeStruct((batch, 6, 6, ZL, 2 * C), BF),
        scratch_shapes=[pltpu.VMEM((12, 12, ZL, C), F32)],
        cost_estimate=pl.CostEstimate(flops=14_000_000_000, bytes_accessed=14_000_000, transcendentals=7_000_000),
        compiler_params=pltpu.CompilerParams(vmem_limit_bytes=60 << 20),
        name="feed",
    )(tok, first, mid_a, mid_b, last, w_up, w_down, w_merge)


def on_device(tokens, w_qkv, w_proj, w_up, w_down, w_merge, earth_bias, position_index, region_ids):
    tok = jnp.transpose(tokens, (0, 2, 3, 1, 4))
    (
        bias, mid_left_a, mid_left_b, mid_right_a, mid_right_b, last_left, last_right, below_left, below_right,
        next_mid_a, prev_mid_a, next_last, prev_last, next_below, prev_below,
    ) = gather(tok, earth_bias, position_index, region_ids)
    last_out, below_out, next_mid_b, prev_mid_b = attend(
        (last_left, below_left, last_right, below_right, next_last, next_below, prev_last, prev_below),
        w_qkv, w_proj, bias, 1, (mid_left_b, mid_right_b),
    )
    mid_a, mid_b = attend(
        (mid_left_a, mid_left_b, mid_right_a, mid_right_b, next_mid_a, next_mid_b, prev_mid_a, prev_mid_b),
        w_qkv, w_proj, bias, 0,
    )
    first_out = passed_along(below_out, "lat", 1)
    merged = feed(tok, first_out, mid_a, mid_b, last_out, w_up, w_down, w_merge)
    return jnp.transpose(merged, (0, 3, 1, 2, 4))


def solution(mesh):
    in_specs = (
        P(None, None, "lat", "lon", None),
        P(),
        P(),
        P(),
        P(),
        P(),
        P("lat", None, None, None),
        P(),
        P("lat", None, None),
    )
    out_specs = P(None, None, "lat", "lon", None)
    return jax.shard_map(
        on_device, mesh=mesh, in_specs=in_specs, out_specs=out_specs, check_vma=False
    )
```

```python
import jax
import jax.numpy as jnp
import numpy as np
from jax import lax
from jax.experimental import pallas as pl
from jax.experimental.pallas import tpu as pltpu
from jax.sharding import PartitionSpec as P

HEADS = 12
HEAD_DIM = 32
C = 384
FFN = 1536
ZL = 8
ZW = 4
HALF = 72
SLOTS = 144
LANES = 256
CELLS = 288
PIECE = 144
LOG2E = 1.4426950408889634
BF = jnp.bfloat16
F32 = jnp.float32


def passed_along(block, axis, distance):
    devices = range(lax.axis_size(axis))
    route = [((i - distance) % len(devices), i) for i in devices]
    return lax.ppermute(block, axis, route)


def normalized(x):
    width = x.shape[-1]
    center = x - jnp.sum(x, axis=-1, keepdims=True) * (1.0 / width)
    spread = jnp.sum(center * center, axis=-1, keepdims=True) * (1.0 / width)
    return center * lax.rsqrt(spread + 1e-05)


def dot(a, b):
    return jnp.dot(a, b, preferred_element_type=F32)


def neighbour(axis, distance):
    size = lax.axis_size(axis)
    return {axis: lax.rem(lax.axis_index(axis) + distance + size, size)}


def remote(source, target, send_sem, recv_sem, axis, distance):
    return pltpu.make_async_remote_copy(
        src_ref=source,
        dst_ref=target,
        send_sem=send_sem,
        recv_sem=recv_sem,
        device_id=neighbour(axis, distance),
        device_id_type=pl.DeviceIdType.MESH,
    )


def greet(axes):
    barrier = pltpu.get_barrier_semaphore()
    for axis in axes:
        for distance in (-1, 1):
            pl.semaphore_signal(
                barrier, inc=1, device_id=neighbour(axis, distance), device_id_type=pl.DeviceIdType.MESH
            )


def greeted(axes):
    pl.semaphore_wait(pltpu.get_barrier_semaphore(), 2 * len(axes))


def full(shape):
    return pl.BlockSpec(shape, lambda *i: (0,) * len(shape))


ROWS_AT_ONCE = 8
STEPS = SLOTS // ROWS_AT_ONCE
TYPE_HEADS = 96
PITCH = 97
TABLE = 3312
ALONG = 4
FORWARD = 10
PICKS = 4


def slot_order():
    return np.arange(SLOTS, dtype=np.int32).reshape(2, 6, 2, 6).transpose(2, 1, 3, 0).reshape(-1)


def gather_kernel(
    index_ref, tok_ref, table_ref, labels_ref, slots_ref,
    out_ref, mid_left_a, mid_left_b, mid_right_a, mid_right_b, last_left, last_right, below_left, below_right,
    next_mid_a, prev_mid_a, next_last, prev_last, next_below, prev_below,
    rows, picked, left, right, region_ref, region_col_ref, mids, firsts, lasts, send_sems, recv_sems, local_sems,
):
    step = pl.program_id(0)

    routes = (
        (firsts.at[0], below_left, "lat", -1),
        (firsts.at[1], below_right, "lat", -1),
        (lasts.at[0], next_last, "lon", -1),
        (lasts.at[1], prev_last, "lon", 1),
        (below_left, next_below, "lon", -1),
        (below_right, prev_below, "lon", 1),
        (mids.at[0, 0], next_mid_a, "lon", -1),
        (mids.at[0, 1], prev_mid_a, "lon", 1),
    )

    def block(n):
        source, target, axis, distance = routes[n]
        return remote(source, target, send_sems.at[n], recv_sems.at[n], axis, distance)

    def local():
        pairs = (
            (mids.at[0, 0], mid_left_a), (mids.at[0, 1], mid_right_a),
            (mids.at[1, 0], mid_left_b), (mids.at[1, 1], mid_right_b),
            (lasts.at[0], last_left), (lasts.at[1], last_right),
        )
        return [pltpu.make_async_copy(a, b, local_sems.at[n]) for n, (a, b) in enumerate(pairs)]

    @pl.when(step == 0)
    def _():
        greet(("lat", "lon"))
        for piece, blocks in ((0, firsts), (3, lasts), (1, mids.at[0]), (2, mids.at[1])):
            for b in range(tok_ref.shape[0]):
                x = normalized(tok_ref[b, 3 * piece : 3 * piece + 3].astype(F32))
                for side in range(2):
                    part = x[:, 6 * side : 6 * side + 6].reshape(PIECE, C).astype(BF)
                    blocks[side, b] = part
            if piece == 0:
                greeted(("lat", "lon"))
                block(0).start()
                block(1).start()
        for copy in local():
            copy.start()
        for c in range(0, TABLE, 128):
            width = min(128, TABLE - c)
            some = table_ref[:, :, :, c : c + width].reshape(TYPE_HEADS, width)
            rows[c : c + width, :TYPE_HEADS] = some.T
        labels = dot((labels_ref[...] + 1).astype(F32).astype(BF), slots_ref[...])
        region_ref[...] = labels
        region_col_ref[...] = labels.T

    @pl.when(step == ALONG)
    def _():
        block(2).start()
        block(3).start()

    @pl.when(step == FORWARD)
    def _():
        for n in range(2):
            block(n).wait_recv()
            block(4 + n).start()
        block(6).start()
        block(7).start()

    order = [int(n) for n in slot_order()]

    def pick(turn, carry):
        for j in range(PICKS):
            row = step * ROWS_AT_ONCE + turn * (PICKS // 2) + j // 2
            side, place = row // HALF, row % HALF
            slot = place % 2 * 72 + place // 12 * 12 + side * 6 + place // 2 % 6
            base = pl.multiple_of(turn * (PICKS * HALF) + j * HALF, 8)
            for k in range(HALF):
                picked[pl.ds(base + k, 1), :] = rows[pl.ds(index_ref[slot, order[j % 2 * HALF + k]], 1), :]
        return carry

    lax.fori_loop(0, ROWS_AT_ONCE * 2 // PICKS, pick, 0)
    for s in range(ROWS_AT_ONCE):
        left[PITCH * s : PITCH * s + TYPE_HEADS, :] = picked[SLOTS * s : SLOTS * s + 128, :].T[:TYPE_HEADS]
        right[PITCH * s : PITCH * s + TYPE_HEADS, :16] = picked[SLOTS * s + 128 : SLOTS * (s + 1), :].T[:TYPE_HEADS]
    for lw in range(2):
        for zw in range(ZW):
            kind = lw * ZW + zw
            same = region_col_ref[pl.ds(pl.multiple_of(step * ROWS_AT_ONCE, 8), ROWS_AT_ONCE), kind : kind + 1] == region_ref[kind : kind + 1, :]
            for h in range(HEADS):
                source = (lw * HEADS + h) * ZW + zw
                place = kind * HEADS + h
                out_ref[0, place, :, :128] = jnp.where(
                    same[:, :128], left[pl.ds(source, ROWS_AT_ONCE, stride=PITCH), :] * LOG2E, -1e9
                )
                out_ref[0, place, :, 128:] = jnp.where(
                    same[:, 128:], right[pl.ds(source, ROWS_AT_ONCE, stride=PITCH), :] * LOG2E, -1e9
                )

    @pl.when(step == STEPS - 1)
    def _():
        for n in range(8):
            block(n).wait_send()
            if n >= 2:
                block(n).wait_recv()
        for copy in local():
            copy.wait()


def gather(tok, earth_bias, position_index, region_ids):
    batch = tok.shape[0]
    table = jnp.transpose(earth_bias, (0, 3, 1, 2))
    slots = np.zeros((SLOTS, LANES), np.float32)
    slots[slot_order(), np.arange(SLOTS)] = 1.0
    one = jax.ShapeDtypeStruct((batch, PIECE, C), BF)
    anywhere = pl.BlockSpec(memory_space=pl.ANY)
    return pl.pallas_call(
        gather_kernel,
        grid=(STEPS,),
        in_specs=[
            pl.BlockSpec(memory_space=pltpu.SMEM),
            full(tok.shape),
            full(table.shape),
            full((2 * ZW, SLOTS)),
            full((SLOTS, LANES)),
        ],
        out_specs=[pl.BlockSpec((1, TYPE_HEADS, ROWS_AT_ONCE, LANES), lambda i: (i, 0, 0, 0))] + [anywhere] * 14,
        out_shape=[jax.ShapeDtypeStruct((STEPS, TYPE_HEADS, ROWS_AT_ONCE, LANES), F32)]
        + [one] * 14,
        scratch_shapes=[
            pltpu.VMEM((TABLE, 128), F32),
            pltpu.VMEM((ROWS_AT_ONCE * SLOTS, 128), F32),
            pltpu.VMEM((ROWS_AT_ONCE * PITCH, 128), F32),
            pltpu.VMEM((ROWS_AT_ONCE * PITCH, 128), F32),
            pltpu.VMEM((2 * ZW, LANES), F32),
            pltpu.VMEM((LANES, 2 * ZW), F32),
            pltpu.VMEM((2, 2, batch, PIECE, C), BF),
            pltpu.VMEM((2, batch, PIECE, C), BF),
            pltpu.VMEM((2, batch, PIECE, C), BF),
            pltpu.SemaphoreType.DMA((8,)),
            pltpu.SemaphoreType.DMA((8,)),
            pltpu.SemaphoreType.DMA((6,)),
        ],
        cost_estimate=pl.CostEstimate(flops=20_000_000, bytes_accessed=100_000_000, transcendentals=0),
        compiler_params=pltpu.CompilerParams(
            collective_id=0, has_side_effects=True, vmem_limit_bytes=60 << 20
        ),
        name="gather",
    )(position_index, tok, table, region_ids.reshape(2 * ZW, SLOTS), jnp.asarray(slots, BF))


def attend_kernel(
    lower_a, lower_b, upper_a, upper_b, right_a, right_b, left_a, left_b, w_qkv_ref, w_proj_ref, *rest
):
    bias_refs, rest = rest[:2], rest[2:]
    if len(rest) > 5:
        mid_left, mid_right, out_a, out_b, next_mid, prev_mid, own_scr, halo_scr, ctx_scr, send_sems, recv_sems = rest

        def blocks():
            return (
                remote(mid_left, next_mid, send_sems.at[0], recv_sems.at[0], "lon", -1),
                remote(mid_right, prev_mid, send_sems.at[1], recv_sems.at[1], "lon", 1),
            )

        @pl.when(pl.program_id(0) == 0)
        def _():
            greet(("lon",))

        @pl.when(pl.program_id(0) == 1)
        def _():
            greeted(("lon",))
            for block in blocks():
                block.start()
    else:
        blocks = None
        out_a, out_b, own_scr, halo_scr, ctx_scr = rest
    level = lax.broadcasted_iota(jnp.int32, (1, ZL, 128), 1)
    level = jnp.concatenate([level] * 3, axis=-1)

    def chosen(parts, which):
        result = parts[0]
        for n in range(1, 4):
            result = jnp.where(which == n, parts[n], result)
        return result

    def windows(top, bottom):
        x = jnp.concatenate([top, bottom], axis=0).astype(F32).reshape(9, 4, ZL, C)
        result = []
        for zw in range(ZW):
            parts = [pltpu.roll(x[:, i], (2 * i - 2 * zw - 1) % ZL, axis=1) for i in range(4)]
            result.append(chosen(parts, level // 2).reshape(HALF, C))
        return jnp.concatenate(result, axis=0).astype(BF)

    def natural(x):
        result = []
        for i in range(4):
            parts = [
                pltpu.roll(x[zw * HALF : (zw + 1) * HALF].reshape(9, ZL, C), (2 * zw + 1 - 2 * i) % ZL, axis=1)
                for zw in range(ZW)
            ]
            result.append(chosen(parts, (level + ZL - 1) % ZL // 2))
        return jnp.stack(result, axis=1).reshape(CELLS, C)

    own = jnp.concatenate([windows(upper_a[0], upper_b[0]), windows(lower_a[0], lower_b[0])], axis=0)
    own_scr[...] = dot(own, w_qkv_ref[...])
    halo = jnp.concatenate([windows(right_a[0], right_b[0]), windows(left_a[0], left_b[0])], axis=0)
    halo_scr[...] = dot(halo, w_qkv_ref[:, C:])
    lane_head = lax.broadcasted_iota(jnp.int32, (1, 128), 1) // HEAD_DIM
    masks = [lane_head == h for h in range(4)]
    ones = jnp.ones((SLOTS, 128), BF)

    for zw in range(ZW):
        for side in range(2):
            rows = slice(side * CELLS + zw * HALF, side * CELLS + (zw + 1) * HALF)
            for g in range(3):
                lanes = slice(128 * g, 128 * g + 128)
                klanes = slice(C + 128 * g, C + 128 * g + 128)
                vlanes = slice(2 * C + 128 * g, 2 * C + 128 * g + 128)
                q = own_scr[rows, lanes] * (HEAD_DIM ** (-0.5) * LOG2E)
                stacked = jnp.concatenate([jnp.where(m, q, 0.0) for m in masks], axis=0).astype(BF)
                k = [own_scr[rows, klanes], halo_scr[rows, lanes]]
                v = [own_scr[rows, vlanes], halo_scr[rows, klanes]]
                if side == 1:
                    k, v = k[::-1], v[::-1]
                keys = jnp.concatenate(k, axis=0).astype(BF)
                values = jnp.concatenate([jnp.concatenate(v, axis=0).astype(BF), ones], axis=1)
                scores = lax.dot_general(stacked, keys, (((1,), (1,)), ((), ())), preferred_element_type=F32)
                bias = jnp.swapaxes(bias_refs[side][:, zw * HEADS + 4 * g : zw * HEADS + 4 * g + 4, :, :SLOTS], 0, 1)
                scores = scores + bias.reshape(4 * HALF, SLOTS)
                raised = jnp.exp2(scores - jnp.max(scores, axis=-1, keepdims=True)).astype(BF)
                both = dot(raised, values)
                top, total = both[:HALF, :128], both[:HALF, 128:]
                for h in range(1, 4):
                    top = jnp.where(masks[h], both[h * HALF : (h + 1) * HALF, :128], top)
                    total = jnp.where(masks[h], both[h * HALF : (h + 1) * HALF, 128:], total)
                ctx_scr[rows, lanes] = top / total
    for side in range(2):
        context = natural(ctx_scr[CELLS * side : CELLS * (side + 1), :]).astype(BF)
        result = dot(context, w_proj_ref[...]).astype(BF)
        out_a[1 - side, 0] = result[:PIECE]
        out_b[1 - side, 0] = result[PIECE:]
    if blocks is not None:

        @pl.when(pl.program_id(0) == pl.num_programs(0) - 1)
        def _():
            for block in blocks():
                block.wait()


def attend(streams, w_qkv, w_proj, bias, lw, travelling=()):
    batch = streams[0].shape[0]
    specs = [pl.BlockSpec((1, PIECE, C), lambda b: (b, 0, 0))] * len(streams)
    anywhere = [pl.BlockSpec(memory_space=pl.ANY)] * len(travelling)
    sems = [pltpu.SemaphoreType.DMA((2,))] * len(travelling)
    remote_params = dict(collective_id=1, has_side_effects=True) if travelling else {}
    out = jax.ShapeDtypeStruct((2, batch, PIECE, C), BF)
    out_spec = pl.BlockSpec((2, 1, PIECE, C), lambda b: (0, b, 0, 0))
    return pl.pallas_call(
        attend_kernel,
        grid=(batch,),
        in_specs=specs
        + [
            full((C, 3 * C)),
            full((C, C)),
            pl.BlockSpec((STEPS // 2, ZW * HEADS, ROWS_AT_ONCE, LANES), lambda b: (0, lw, 0, 0)),
            pl.BlockSpec((STEPS // 2, ZW * HEADS, ROWS_AT_ONCE, LANES), lambda b: (1, lw, 0, 0)),
        ]
        + anywhere,
        out_specs=[out_spec, out_spec] + anywhere,
        out_shape=[out, out] + [jax.ShapeDtypeStruct(array.shape, BF) for array in travelling],
        scratch_shapes=[
            pltpu.VMEM((2 * CELLS, 3 * C), F32),
            pltpu.VMEM((2 * CELLS, 2 * C), F32),
            pltpu.VMEM((2 * CELLS, C), F32),
        ]
        + sems,
        cost_estimate=pl.CostEstimate(flops=20_000_000_000, bytes_accessed=16_000_000, transcendentals=4_000_000),
        compiler_params=pltpu.CompilerParams(vmem_limit_bytes=60 << 20, **remote_params),
        name="attend",
    )(*streams, w_qkv, w_proj, bias, bias, *travelling)


CHUNK = 768


def feed_kernel(tok_ref, first_ref, mid_a, mid_b, last_ref, w_up_ref, w_down_ref, w_merge_ref, out_ref, hidden_scr):
    for piece, ref in enumerate((first_ref, mid_a, mid_b, last_ref)):
        for side in range(2):
            rows, cols = slice(3 * piece, 3 * piece + 3), slice(6 * side, 6 * side + 6)
            tok = tok_ref[0, rows, cols].astype(F32)
            attended = ref[side, 0].astype(F32).reshape(3, 6, ZL, C)
            hidden_scr[rows, cols] = (tok + attended).astype(BF).astype(F32)

    hidden = hidden_scr[...].reshape(12 * 12 * ZL, C)
    normed = normalized(hidden).astype(BF)
    block = hidden
    for f in range(0, FFN, CHUNK):
        up = dot(normed, w_up_ref[:, f : f + CHUNK])
        inner = (0.5 * up * (1.0 + lax.erf(up * 0.7071067811865476))).astype(BF)
        block = block + dot(inner, w_down_ref[f : f + CHUNK])
    block = block.astype(BF).astype(F32).reshape(6, 2, 6, 2, ZL, C)
    grouped = jnp.concatenate([block[:, p // 2, :, p % 2] for p in range(4)], axis=-1)
    grouped = normalized(grouped.reshape(36 * ZL, 4 * C)).astype(BF)
    out_ref[0] = dot(grouped, w_merge_ref[...]).reshape(6, 6, ZL, 2 * C).astype(BF)


def feed(tok, first, mid_a, mid_b, last, w_up, w_down, w_merge):
    batch = tok.shape[0]
    piece = pl.BlockSpec((2, 1, PIECE, C), lambda b: (0, b, 0, 0))
    return pl.pallas_call(
        feed_kernel,
        grid=(batch,),
        in_specs=[
            pl.BlockSpec((1, 12, 12, ZL, C), lambda b: (b, 0, 0, 0, 0)),
            piece,
            piece,
            piece,
            piece,
            full((C, FFN)),
            full((FFN, C)),
            full((4 * C, 2 * C)),
        ],
        out_specs=pl.BlockSpec((1, 6, 6, ZL, 2 * C), lambda b: (b, 0, 0, 0, 0)),
        out_shape=jax.ShapeDtypeStruct((batch, 6, 6, ZL, 2 * C), BF),
        scratch_shapes=[pltpu.VMEM((12, 12, ZL, C), F32)],
        cost_estimate=pl.CostEstimate(flops=14_000_000_000, bytes_accessed=14_000_000, transcendentals=7_000_000),
        compiler_params=pltpu.CompilerParams(vmem_limit_bytes=60 << 20),
        name="feed",
    )(tok, first, mid_a, mid_b, last, w_up, w_down, w_merge)


def on_device(tokens, w_qkv, w_proj, w_up, w_down, w_merge, earth_bias, position_index, region_ids):
    tok = jnp.transpose(tokens, (0, 2, 3, 1, 4))
    (
        bias, mid_left_a, mid_left_b, mid_right_a, mid_right_b, last_left, last_right, below_left, below_right,
        next_mid_a, prev_mid_a, next_last, prev_last, next_below, prev_below,
    ) = gather(tok, earth_bias, position_index, region_ids)
    last_out, below_out, next_mid_b, prev_mid_b = attend(
        (last_left, below_left, last_right, below_right, next_last, next_below, prev_last, prev_below),
        w_qkv, w_proj, bias, 1, (mid_left_b, mid_right_b),
    )
    mid_a, mid_b = attend(
        (mid_left_a, mid_left_b, mid_right_a, mid_right_b, next_mid_a, next_mid_b, prev_mid_a, prev_mid_b),
        w_qkv, w_proj, bias, 0,
    )
    first_out = passed_along(below_out, "lat", 1)
    merged = feed(tok, first_out, mid_a, mid_b, last_out, w_up, w_down, w_merge)
    return jnp.transpose(merged, (0, 3, 1, 2, 4))


def solution(mesh):
    in_specs = (
        P(None, None, "lat", "lon", None),
        P(),
        P(),
        P(),
        P(),
        P(),
        P("lat", None, None, None),
        P(),
        P("lat", None, None),
    )
    out_specs = P(None, None, "lat", "lon", None)
    return jax.shard_map(
        on_device, mesh=mesh, in_specs=in_specs, out_specs=out_specs, check_vma=False
    )
```
